256 devices in a mesh: dp: 8 (over x, core), ctx: 32 (over z, y).
Axes of the slice: x: 4, y: 4, z: 8, core: 2. Of those that a mesh axis runs over, the one named last changes fastest.
Arguments:
- queries: bfloat16 [65536, 256], P(('dp', 'ctx')), parts along dimension 0, may hold values from -6 to 6
- keys: bfloat16 [65536, 256], P(('dp', 'ctx')), parts along dimension 0, may hold values from -6 to 6
- values: bfloat16 [65536, 256], P(('dp', 'ctx')), parts along dimension 0, may hold values from -6 to 6
- document_ids: int32 [65536], P(('dp', 'ctx')), parts along dimension 0, may hold values from 0 to 3, never falling along the last dimension, each value on 1 to 4096 neighbouring positions
- output_weight: bfloat16 [256, 4096], P(None, 'ctx'), may hold values from -0.375 to 0.375
Outputs:
- projected: bfloat16 [65536, 4096], P(('dp', 'ctx')), parts along dimension 0
- log_normalizer: float32 [2, 65536], P(None, ('dp', 'ctx')), parts along dimension 1
The draws below stay inside these ranges and needn't reach their ends.
There are 8 independent parts, one for each index of `dp`. The reference program is written for one: setup_inputs(seed, part) draws one part's arguments, and reference() takes and returns one part's arrays. A program takes and returns all parts, laid end to end along the dimension named above; an argument that names none is the same for every part. Nothing has to cross between parts.
Inputs may be any that keep to these rules, and one draw needn't show every extreme that they name: `document_ids`: document numbers never fall along the sequence; no document is longer than 4096 tokens, and one is exactly that long.
All inputs are finite; a program needn't handle non-finite values.
Results may differ from the reference program's by a relative error of at most 0.007.
Values may be sent and summed in bfloat16 or wider, within the bound.
A program may use at most 64 MiB of HBM per device.

```python
import math
import jax
import jax.numpy as jnp
import numpy as np
from jax import lax

D = 4096
HEAD_DIM = 128
HEADS = 2
DOCS = 4
SEQ = 8192


def draw_queries(key, part):
    key = jax.random.fold_in(key, 11)
    matrix = jnp.clip(jax.random.normal(key, (SEQ, HEADS * HEAD_DIM), jnp.float32), -4.5, 4.5)
    return matrix.astype(jnp.bfloat16)


def draw_keys(key, part):
    key = jax.random.fold_in(key, 12)
    matrix = jnp.clip(jax.random.normal(key, (SEQ, HEADS * HEAD_DIM), jnp.float32), -4.5, 4.5)
    return matrix.astype(jnp.bfloat16)


def levels(key, shape, shards, low, largest):
    factor_of = 1.0
    for dim, shards_of in shards:
        heights = jax.random.uniform(jax.random.fold_in(jax.random.fold_in(key, 6), dim), (shards_of,), jnp.float32, low / len(shards), largest / len(shards))
        factor_of = factor_of * jnp.repeat(jnp.exp(heights), shape[dim] // shards_of).reshape((-1,) + (1,) * (len(shape) - 1 - dim))
    return factor_of


def length_profile(count, total, bound, slope):
    portions = [(1 << 20) // math.isqrt(rank ** slope) + 1 for rank in range(2, count + 1)]
    spare, holding = total - bound - (count - 1), [1] * (count - 1)
    while spare > 0:
        free = [i for i in range(count - 1) if holding[i] < bound]
        whole, budget = sum([portions[i] for i in free]), spare
        for i in free:
            extra = min(bound - holding[i], max(1, budget * portions[i] // whole), spare)
            holding[i] = holding[i] + extra
            spare = spare - extra
    return np.array([bound] + holding)


def uneven_parts(own_key, count, total, reach, lean):
    if count == 2:
        one = jax.random.randint(own_key, (), max(1, total - reach), min(reach, total - 1) + 1)
        return jnp.stack([one, total - one])
    lengths = jnp.asarray(length_profile(count, total, reach, lean), jnp.int32)
    couples = (count - 1) // 2
    donor, sink = lengths[1:1 + 2 * couples:2], lengths[2:2 + 2 * couples:2]
    margin = jnp.minimum(donor - 1, reach - sink)
    moved = jax.random.randint(jax.random.fold_in(own_key, 1), (couples,), 0, 1 << 20) % (margin + 1)
    lengths = lengths.at[1:1 + 2 * couples:2].set(donor - moved).at[2:2 + 2 * couples:2].set(sink + moved)
    return lengths[jax.random.permutation(jax.random.fold_in(own_key, 2), count)]


def bell_draw(rng, dims, deviation, limit, cuts=(), held_as=jnp.bfloat16):
    array = jax.random.normal(rng, dims, jnp.float32) * deviation
    if len(cuts) > 0:
        array = levels(rng, dims, cuts, -0.22, 0.18) * array
    return jnp.clip(array, min=-limit, max=limit).astype(held_as)


def setup_inputs(seed: int = 0, part: int = 0) -> dict:
    arg_keys = jax.random.split(jax.random.key(seed), 6)
    own_keys = jax.random.split(jax.random.fold_in(arg_keys[5], part), 6)
    queries = draw_queries(jax.random.fold_in(jax.random.fold_in(arg_keys[5], part), 71), part)
    keys = draw_keys(jax.random.fold_in(jax.random.fold_in(arg_keys[5], part), 71), part)
    values = bell_draw(own_keys[2], (SEQ, HEADS * HEAD_DIM), 1.0, 6.0, ((0, 32),))
    document_ids = jnp.searchsorted(jnp.cumsum(uneven_parts(own_keys[3], DOCS, SEQ, SEQ // 2, 1)), jnp.arange(SEQ), side="right").astype(jnp.int32)
    output_weight = bell_draw(arg_keys[4], (HEADS * HEAD_DIM, D), (HEADS * HEAD_DIM) ** -0.5, 0.375, ((1, 32),))
    return dict(queries=queries, keys=keys, values=values, document_ids=document_ids, output_weight=output_weight)


def reference(queries, keys, values, document_ids, output_weight):
    total_rows = queries.shape[0]
    feature_count = queries.shape[1]
    head_dim = feature_count // HEADS
    score_scale = 1.0 / math.sqrt(head_dim)
    query_heads = queries.astype(jnp.float32).reshape(total_rows, HEADS, head_dim)
    key_heads = keys.astype(jnp.float32).reshape(total_rows, HEADS, head_dim)
    value_heads = values.astype(jnp.float32).reshape(total_rows, HEADS, head_dim)
    positions = jnp.arange(total_rows, dtype=jnp.int32)
    block_rows = math.gcd(total_rows, 512)
    block_starts = jnp.arange(0, total_rows, block_rows, dtype=jnp.int32)

    def one_block(first_row):
        query_block = lax.dynamic_slice_in_dim(query_heads, first_row, block_rows, 0)
        query_pos = lax.dynamic_slice_in_dim(positions, first_row, block_rows, 0)
        query_doc = lax.dynamic_slice_in_dim(document_ids, first_row, block_rows, 0)
        scores = jnp.einsum('qhd,khd->hqk', query_block, key_heads) * score_scale
        visible = (positions[None, :] <= query_pos[:, None]) & (document_ids[None, :] == query_doc[:, None])
        row_max = lax.optimization_barrier(jnp.max(jnp.where(visible[None], scores, -jnp.inf), axis=2))
        weights = jnp.where(visible[None], jnp.exp(scores - row_max[:, :, None]), 0.0)
        row_sum = lax.optimization_barrier(jnp.sum(weights, axis=2))
        rounded = lax.optimization_barrier(weights.astype(jnp.bfloat16)).astype(jnp.float32)
        product = jnp.einsum('hqk,khd->qhd', rounded, value_heads)
        normalized = product / row_sum.T[:, :, None]
        attended_block = normalized.reshape(block_rows, feature_count).astype(jnp.bfloat16)
        return (attended_block, row_max + jnp.log(row_sum))
    attended_blocks, log_blocks = lax.map(one_block, block_starts)
    attended = attended_blocks.reshape(total_rows, feature_count)
    log_normalizer = jnp.transpose(log_blocks, (1, 0, 2)).reshape(HEADS, total_rows)
    projected = jnp.dot(attended, output_weight, preferred_element_type=jnp.float32).astype(jnp.bfloat16)
    return (projected, log_normalizer)
```

```python
import math

import jax
import jax.numpy as jnp
from jax import lax
from jax.experimental import pallas as pl
from jax.experimental.pallas import tpu as pltpu
from jax.sharding import PartitionSpec as P

MESH = pl.DeviceIdType.MESH
HEADS = 2
HEAD_DIM = 128
NX, NC, NZ, NY = 4, 2, 8, 4
ROWS = 256
FEATURES = HEADS * HEAD_DIM
MODEL = 4096
PARTS = NX * NC
PIECE = FEATURES // PARTS
REACH = 4
MASKED = -1e30
SCALE = 1.0 / math.sqrt(HEAD_DIM)
SCALE2 = SCALE * math.log2(math.e)
ARRIVALS = [(h, k) for k in range(1, REACH + 1) for h in range(HEADS)]


def attend_kernel(
    q_in, k_in, v_in, doc_in, w_in,
    out_ref, lse_ref,
    q_all, k_all, vt_all, v_own, doc_q, doc_k, key_doc,
    acc, stat, o_send, o_recv, stat_recv, att, w_all, stage,
    loc_sem, out_sem,
    kv_ss, kv_rs, q_ss, q_rs, dy_ss, dy_rs, dz_ss, dz_rs,
    w1_ss, w1_rs, w2_ss, w2_rs, w3_ss, w3_rs, w4_ss, w4_rs,
    o_ss, o_rs, s_ss, s_rs,
):
    dp = lax.axis_index("dp")
    ctx = lax.axis_index("ctx")
    x, core = dp // NC, lax.rem(dp, NC)
    z, y = ctx // NY, lax.rem(ctx, NY)

    def at(dx=0, flip=False, dz=0, dy=0):
        x_to = lax.rem(x + dx + NX, NX)
        core_to = 1 - core if flip else core
        z_to = lax.rem(z + dz + NZ, NZ)
        y_to = lax.rem(y + dy + NY, NY)
        return (x_to * NC + core_to, z_to * NY + y_to)

    def remote(src, dst, ss, rs, to):
        return pltpu.make_async_remote_copy(
            src_ref=src, dst_ref=dst, send_sem=ss, recv_sem=rs, device_id=to, device_id_type=MESH
        )

    barrier = pltpu.get_barrier_semaphore()
    partners = [at(dz=d) for d in range(1, NZ)]
    partners += [at(dy=d) for d in range(1, NY)]
    partners += [at(dx=d) for d in range(1, NX)]
    partners += [at(flip=True)]
    for to in partners:
        pl.semaphore_signal(barrier, inc=1, device_id=to, device_id_type=MESH)

    piece = pl.ds(pl.multiple_of(dp * PIECE, PIECE), PIECE)
    z_cols = pl.ds(pl.multiple_of(z * 128, 128), 128)
    locals_ = [
        pltpu.make_async_copy(v_in, v_own, loc_sem.at[0]),
        pltpu.make_async_copy(k_in.at[:, 0:128], k_all.at[0, 0], loc_sem.at[1]),
        pltpu.make_async_copy(k_in.at[:, 128:256], k_all.at[0, 1], loc_sem.at[2]),
        pltpu.make_async_copy(q_in, q_all.at[0], loc_sem.at[3]),
        pltpu.make_async_copy(doc_in, doc_q.at[0], loc_sem.at[4]),
        pltpu.make_async_copy(w_in.at[piece], w_all.at[y, piece, z_cols], loc_sem.at[5]),
    ]
    for copy in locals_:
        copy.start()
    locals_[0].wait()
    v_turned = v_own[...].T
    for h in range(HEADS):
        vt_all[0, h] = v_turned[h * HEAD_DIM : (h + 1) * HEAD_DIM]
    for copy in locals_[1:]:
        copy.wait()

    def kv_copy(h, k, part):
        ref = (k_all, vt_all)[part]
        return remote(
            ref.at[k, h], ref.at[k + 1, h],
            kv_ss.at[h, k, part], kv_rs.at[h, k, part], at(dz=1),
        )

    def forward(h, k, part):
        @pl.when((z >= k) & (z < NZ - 1))
        def _():
            kv_copy(h, k, part).start()

    q_copies = [
        remote(q_in, q_all.at[d], q_ss.at[d - 1], q_rs.at[d - 1], at(dy=d)) for d in range(1, NY)
    ]
    dy_copies = [
        remote(doc_in, doc_q.at[d], dy_ss.at[d - 1], dy_rs.at[d - 1], at(dy=d))
        for d in range(1, NY)
    ]
    dz_copies = [
        remote(doc_in, doc_k.at[k - 1], dz_ss.at[k - 1], dz_rs.at[k - 1], at(dz=k))
        for k in range(1, REACH + 1)
    ]
    own_piece = w_all.at[y, piece, z_cols]
    w1_copies = [
        remote(own_piece, own_piece, w1_ss.at[d - 1], w1_rs.at[d - 1], at(dz=d))
        for d in range(1, NZ)
    ]
    own_column = w_all.at[y, piece]
    w2_copies = [
        remote(own_column, own_column, w2_ss.at[d - 1], w2_rs.at[d - 1], at(dy=d))
        for d in range(1, NY)
    ]
    own_rows = w_all.at[:, piece]
    w3_copies = [
        remote(own_rows, own_rows, w3_ss.at[d - 1], w3_rs.at[d - 1], at(dx=d))
        for d in range(1, NX)
    ]

    def part_rows(d):
        part = lax.rem(x - d + NX, NX) * NC + core
        return w_all.at[:, pl.ds(pl.multiple_of(part * PIECE, PIECE), PIECE)]

    w4_copies = [
        remote(part_rows(d), part_rows(d), w4_ss.at[d], w4_rs.at[d], at(flip=True))
        for d in range(NX)
    ]
    o_copies = [
        [
            remote(o_send.at[h, d - 1], o_recv.at[h, d - 1], o_ss.at[h, d - 1], o_rs.at[h, d - 1], at(dy=-d))
            for d in range(1, NY)
        ]
        for h in range(HEADS)
    ]
    s_copies = [
        [
            remote(stat.at[d, h], stat_recv.at[h, d - 1], s_ss.at[h, d - 1], s_rs.at[h, d - 1], at(dy=-d))
            for d in range(1, NY)
        ]
        for h in range(HEADS)
    ]

    def turned_docs(row):
        return jnp.broadcast_to(row, (128, ROWS)).T

    key_doc[0] = turned_docs(doc_q[0])

    pl.semaphore_wait(barrier, len(partners))

    for h in range(HEADS):
        for part in range(2):
            forward(h, 0, part)
    for copy in q_copies + dy_copies:
        copy.start()
    for k in range(1, REACH + 1):
        @pl.when(z + k < NZ)
        def _(k=k):
            dz_copies[k - 1].start()
    for copy in w1_copies:
        copy.start()

    def tile(h, k, d, first, causal):
        scores = lax.dot_general(
            k_all[k, h], q_all[d, :, h * HEAD_DIM : (h + 1) * HEAD_DIM],
            (((1,), (1,)), ((), ())), preferred_element_type=jnp.float32,
        )
        kd = key_doc[k]
        visible = jnp.concatenate([kd, kd], axis=1) == doc_q[d]
        if causal:
            key_row = lax.broadcasted_iota(jnp.int32, (ROWS, ROWS), 0) + y * ROWS
            query_row = lax.broadcasted_iota(jnp.int32, (ROWS, ROWS), 1) + lax.rem(y - d + NY, NY) * ROWS
            visible = visible & (key_row <= query_row)
        scores = jnp.where(visible, scores, MASKED)
        top = jnp.max(scores, axis=0, keepdims=True)
        if not first:
            old = stat[d, h, 0:1]
            top = jnp.maximum(top, old)
        weights = jnp.exp2((scores - top) * SCALE2)
        total = jnp.sum(weights, axis=0, keepdims=True)
        product = jnp.dot(
            vt_all[k, h], weights.astype(jnp.bfloat16), preferred_element_type=jnp.float32
        )
        if not first:
            fade = jnp.exp2((old - top) * SCALE2)
            total = total + stat[d, h, 1:2] * fade
            product = product + acc[d, h] * fade
        stat[d, h, 0:1] = top
        stat[d, h, 1:2] = total
        acc[d, h] = product

    def tiles(h, k):
        def body(d, carry):
            tile(h, k, d, k == 0, k == 0)
            return carry
        lax.fori_loop(0, NY, body, 0)

    def give_back(h):
        for d in range(1, NY):
            o_send[h, d - 1] = acc[d, h].astype(jnp.bfloat16)
            o_copies[h][d - 1].start()
            s_copies[h][d - 1].start()

    for h in range(HEADS):
        tile(h, 0, 0, True, True)
    for d in range(1, NY):
        q_copies[d - 1].wait_recv()
        dy_copies[d - 1].wait_recv()
    for h in range(HEADS):
        def early(d, carry, h=h):
            tile(h, 0, d, True, True)
            return carry
        lax.fori_loop(1, NY, early, 0)

    for step, (h, k) in enumerate(ARRIVALS):
        @pl.when(z >= k)
        def _(h=h, k=k):
            kv_copy(h, k - 1, 0).wait_recv()
            if k < REACH:
                forward(h, k, 0)
            kv_copy(h, k - 1, 1).wait_recv()
            if k < REACH:
                forward(h, k, 1)
            if h == 0:
                dz_copies[k - 1].wait_recv()
                key_doc[k] = turned_docs(doc_k[k - 1])
            tiles(h, k)
        if k == REACH:
            give_back(h)
        if step == 0:
            for copy in w1_copies:
                copy.wait_recv()
            for copy in w2_copies:
                copy.start()
        if step == 2:
            for copy in w2_copies:
                copy.wait_recv()
            for copy in w3_copies:
                copy.start()
            w4_copies[0].start()

    for d in range(1, NX):
        w3_copies[d - 1].wait_recv()
        w4_copies[d].start()

    for h in range(HEADS):
        for d in range(1, NY):
            o_copies[h][d - 1].wait_recv()
            s_copies[h][d - 1].wait_recv()
        tops = [stat[0, h, 0:1]] + [stat_recv[h, d, 0:1] for d in range(NY - 1)]
        sums = [stat[0, h, 1:2]] + [stat_recv[h, d, 1:2] for d in range(NY - 1)]
        top = tops[0]
        for other in tops[1:]:
            top = jnp.maximum(top, other)
        shares = [jnp.exp2((one - top) * SCALE2) for one in tops]
        total = sums[0] * shares[0]
        value = acc[0, h] * shares[0]
        for d in range(1, NY):
            total = total + sums[d] * shares[d]
            value = value + o_recv[h, d - 1].astype(jnp.float32) * shares[d]
        lse_ref[h : h + 1] = top * SCALE + jnp.log(total)
        value = value / total
        att[:, h * HEAD_DIM : (h + 1) * HEAD_DIM] = value.T.astype(jnp.bfloat16)

    for copy in w4_copies:
        copy.wait_recv()
    attended = att[...]
    writes = []
    width = NY * 128
    for block in range(NZ):
        weight = jnp.concatenate(
            [w_all[c, :, block * 128 : (block + 1) * 128] for c in range(NY)], axis=1
        )
        cols = slice(block * width, (block + 1) * width)
        stage[:, cols] = jnp.dot(
            attended, weight, preferred_element_type=jnp.float32
        ).astype(jnp.bfloat16)
        write = pltpu.make_async_copy(stage.at[:, cols], out_ref.at[:, cols], out_sem.at[block])
        write.start()
        writes.append(write)

    for h, k in [(h, k) for k in range(REACH) for h in range(HEADS)]:
        @pl.when((z >= k) & (z < NZ - 1))
        def _(h=h, k=k):
            for part in range(2):
                kv_copy(h, k, part).wait_send()
    for copy in q_copies + dy_copies + w1_copies + w2_copies + w3_copies + w4_copies:
        copy.wait_send()
    for k in range(1, REACH + 1):
        @pl.when(z + k < NZ)
        def _(k=k):
            dz_copies[k - 1].wait_send()
    for h in range(HEADS):
        for copy in o_copies[h] + s_copies[h]:
            copy.wait_send()
    for write in writes:
        write.wait()


def on_device(queries, keys, values, document_ids, output_weight):
    bf16, f32, i32 = jnp.bfloat16, jnp.float32, jnp.int32
    dma = pltpu.SemaphoreType.DMA
    anywhere = pl.BlockSpec(memory_space=pl.ANY)
    return pl.pallas_call(
        attend_kernel,
        out_shape=(
            jax.ShapeDtypeStruct((ROWS, MODEL), bf16),
            jax.ShapeDtypeStruct((HEADS, ROWS), f32),
        ),
        in_specs=[anywhere] * 5,
        out_specs=(anywhere, pl.BlockSpec(memory_space=pltpu.VMEM)),
        scratch_shapes=[
            pltpu.VMEM((NY, ROWS, FEATURES), bf16),
            pltpu.VMEM((REACH + 1, HEADS, ROWS, HEAD_DIM), bf16),
            pltpu.VMEM((REACH + 1, HEADS, HEAD_DIM, ROWS), bf16),
            pltpu.VMEM((ROWS, FEATURES), bf16),
            pltpu.VMEM((NY, 1, ROWS), i32),
            pltpu.VMEM((REACH, 1, ROWS), i32),
            pltpu.VMEM((REACH + 1, ROWS, 128), i32),
            pltpu.VMEM((NY, HEADS, HEAD_DIM, ROWS), f32),
            pltpu.VMEM((NY, HEADS, 2, ROWS), f32),
            pltpu.VMEM((HEADS, NY - 1, HEAD_DIM, ROWS), bf16),
            pltpu.VMEM((HEADS, NY - 1, HEAD_DIM, ROWS), bf16),
            pltpu.VMEM((HEADS, NY - 1, 2, ROWS), f32),
            pltpu.VMEM((ROWS, FEATURES), bf16),
            pltpu.VMEM((NY, FEATURES, NZ * 128), bf16),
            pltpu.VMEM((ROWS, MODEL), bf16),
            dma((6,)), dma((NZ,)),
            dma((HEADS, REACH, 2)), dma((HEADS, REACH, 2)),
            dma((NY - 1,)), dma((NY - 1,)), dma((NY - 1,)), dma((NY - 1,)),
            dma((REACH,)), dma((REACH,)),
            dma((NZ - 1,)), dma((NZ - 1,)), dma((NY - 1,)), dma((NY - 1,)),
            dma((NX - 1,)), dma((NX - 1,)), dma((NX,)), dma((NX,)),
            dma((HEADS, NY - 1)), dma((HEADS, NY - 1)),
            dma((HEADS, NY - 1)), dma((HEADS, NY - 1)),
        ],
        compiler_params=pltpu.CompilerParams(
            collective_id=0, has_side_effects=True, vmem_limit_bytes=32 << 20
        ),
    )(queries, keys, values, document_ids.reshape(1, ROWS), output_weight)


def solution(mesh):
    in_specs = (
        P(("dp", "ctx"), None),
        P(("dp", "ctx"), None),
        P(("dp", "ctx"), None),
        P(("dp", "ctx")),
        P(None, "ctx"),
    )
    out_specs = (P(("dp", "ctx"), None), P(None, ("dp", "ctx")))
    return jax.shard_map(
        on_device, mesh=mesh, in_specs=in_specs, out_specs=out_specs, check_vma=False
    )
```

```python
import math

import jax
import jax.numpy as jnp
from jax import lax
from jax.experimental import pallas as pl
from jax.experimental.pallas import tpu as pltpu
from jax.sharding import PartitionSpec as P

MESH = pl.DeviceIdType.MESH
HEADS = 2
HEAD_DIM = 128
NX, NC, NZ, NY = 4, 2, 8, 4
ROWS = 256
HALF = 128
FEATURES = HEADS * HEAD_DIM
MODEL = 4096
PARTS = NX * NC
PIECE = FEATURES // PARTS
REACH = 4
MASKED = -1e30
SCALE = 1.0 / math.sqrt(HEAD_DIM)
SCALE2 = SCALE * math.log2(math.e)
AROUND = [(0, 0), (1, 0)]
JUMP = 2


def attend_kernel(
    q_in, k_in, v_in, doc_in, w_in,
    att, w_all, lse_ref,
    q_all, k_all, vt_all, v_own, doc_q, doc_k, key_doc,
    acc, stat, o_send, o_recv, stat_recv, relay_k, relay_v,
    loc_sem,
    kv_ss, kv_rs, a_ss, a_rs, b_ss, q_ss, q_rs, dy_ss, dy_rs, dz_ss, dz_rs,
    w1_ss, w1_rs, w2_ss, w2_rs, w3_ss, w3_rs, w4_ss, w4_rs,
    o_ss, o_rs, s_ss, s_rs,
):
    dp = lax.axis_index("dp")
    ctx = lax.axis_index("ctx")
    x, core = dp // NC, lax.rem(dp, NC)
    z, y = ctx // NY, lax.rem(ctx, NY)

    def at(dx=0, flip=False, dz=0, dy=0):
        x_to = lax.rem(x + dx + NX, NX)
        core_to = 1 - core if flip else core
        z_to = lax.rem(z + dz + NZ, NZ)
        y_to = lax.rem(y + dy + NY, NY)
        return (x_to * NC + core_to, z_to * NY + y_to)

    def remote(src, dst, ss, rs, to):
        return pltpu.make_async_remote_copy(
            src_ref=src, dst_ref=dst, send_sem=ss, recv_sem=rs, device_id=to, device_id_type=MESH
        )

    barrier = pltpu.get_barrier_semaphore()
    partners = [at(dz=d) for d in range(1, NZ)]
    partners += [at(dy=d) for d in range(1, NY)]
    partners += [at(dx=d) for d in range(1, NX)]
    partners += [at(flip=True)]
    for to in partners:
        pl.semaphore_signal(barrier, inc=1, device_id=to, device_id_type=MESH)

    piece = pl.ds(pl.multiple_of(dp * PIECE, PIECE), PIECE)
    z_cols = pl.ds(pl.multiple_of(z * 128, 128), 128)
    locals_ = [
        pltpu.make_async_copy(v_in, v_own, loc_sem.at[0]),
        pltpu.make_async_copy(k_in.at[:, 0:128], k_all.at[0, 0], loc_sem.at[1]),
        pltpu.make_async_copy(k_in.at[:, 128:256], k_all.at[0, 1], loc_sem.at[2]),
        pltpu.make_async_copy(q_in, q_all.at[0], loc_sem.at[3]),
        pltpu.make_async_copy(doc_in, doc_q.at[0], loc_sem.at[4]),
        pltpu.make_async_copy(w_in.at[piece], w_all.at[y, piece, z_cols], loc_sem.at[5]),
    ]
    for copy in locals_:
        copy.start()
    locals_[0].wait()
    v_turned = v_own[...].T
    for h in range(HEADS):
        vt_all[0, h] = v_turned[h * HEAD_DIM : (h + 1) * HEAD_DIM]
    for copy in locals_[1:]:
        copy.wait()

    def kv_copy(h, k, part):
        ref = (k_all, vt_all)[part]
        return remote(
            ref.at[k, h], ref.at[k + 1, h],
            kv_ss.at[h, k, part], kv_rs.at[h, k, part], at(dz=1),
        )

    def advance(h, k, part):
        @pl.when(z >= k)
        def _():
            kv_copy(h, k - 1, part).wait_recv()

        last = REACH - 2 if (h, part) in AROUND else REACH - 1

        @pl.when((z >= k) & (z < NZ - 1) & (k <= last))
        def _():
            kv_copy(h, k, part).start()

    def around_out(h, part):
        return remote(
            (k_all, vt_all)[part].at[0, h], (relay_k, relay_v)[part].at[h],
            a_ss.at[h, part], a_rs.at[h, part], at(dz=-JUMP),
        )

    def around_in(h, part):
        return remote(
            (relay_k, relay_v)[part].at[h], (k_all, vt_all)[part].at[REACH, h],
            b_ss.at[h, part], kv_rs.at[h, REACH - 1, part], at(dz=-JUMP),
        )

    sends_around = z < NZ - REACH
    relays_around = (z < NZ - REACH - JUMP) | (z >= NZ - JUMP)

    def relay_around(h, part):
        @pl.when(relays_around)
        def _():
            around_out(h, part).wait_recv()
            around_in(h, part).start()

    q_copies = [
        remote(q_in, q_all.at[d], q_ss.at[d - 1], q_rs.at[d - 1], at(dy=d)) for d in range(1, NY)
    ]
    dy_copies = [
        remote(doc_in, doc_q.at[d], dy_ss.at[d - 1], dy_rs.at[d - 1], at(dy=d))
        for d in range(1, NY)
    ]
    dz_copies = [
        remote(doc_in, doc_k.at[k - 1], dz_ss.at[k - 1], dz_rs.at[k - 1], at(dz=k))
        for k in range(1, REACH + 1)
    ]
    own_piece = w_all.at[y, piece, z_cols]
    w1_copies = [
        remote(own_piece, own_piece, w1_ss.at[d - 1], w1_rs.at[d - 1], at(dz=d))
        for d in range(1, NZ)
    ]
    own_column = w_all.at[y, piece]
    w2_copies = [
        remote(own_column, own_column, w2_ss.at[d - 1], w2_rs.at[d - 1], at(dy=d))
        for d in range(1, NY)
    ]

    def part_rows(dy, dx):
        part = lax.rem(x - dx + NX, NX) * NC + core
        rows = pl.ds(pl.multiple_of(part * PIECE, PIECE), PIECE)
        return w_all.at[lax.rem(y - dy + NY, NY), rows]

    w3_copies = [
        [
            remote(part_rows(dy, 0), part_rows(dy, 0), w3_ss.at[dy, d - 1], w3_rs.at[dy, d - 1], at(dx=d))
            for d in range(1, NX)
        ]
        for dy in range(NY)
    ]
    w4_copies = [
        [
            remote(part_rows(dy, d), part_rows(dy, d), w4_ss.at[dy, d], w4_rs.at[dy, d], at(flip=True))
            for d in range(NX)
        ]
        for dy in range(NY)
    ]

    def weight_over_y():
        for copy in w1_copies:
            copy.wait_recv()
        for copy in w3_copies[0] + w2_copies:
            copy.start()
        w4_copies[0][0].start()

    def weight_over_x():
        for d in range(1, NY):
            w2_copies[d - 1].wait_recv()
            for copy in w3_copies[d]:
                copy.start()
            w4_copies[d][0].start()

    def weight_over_core(dy):
        for d in range(1, NX):
            w3_copies[dy][d - 1].wait_recv()
            w4_copies[dy][d].start()

    o_copies = [
        [
            remote(o_send.at[h, d - 1], o_recv.at[h, d - 1], o_ss.at[h, d - 1], o_rs.at[h, d - 1], at(dy=-d))
            for d in range(1, NY)
        ]
        for h in range(HEADS)
    ]
    s_copies = [
        [
            remote(stat.at[d, h], stat_recv.at[h, d - 1], s_ss.at[h, d - 1], s_rs.at[h, d - 1], at(dy=-d))
            for d in range(1, NY)
        ]
        for h in range(HEADS)
    ]

    def turned_docs(row):
        return jnp.broadcast_to(row, (128, ROWS)).T

    def half_tile(h, k, d, cols, causal):
        scores = lax.dot_general(
            k_all[k, h], q_all[d, cols, h * HEAD_DIM : (h + 1) * HEAD_DIM],
            (((1,), (1,)), ((), ())), preferred_element_type=jnp.float32,
        )
        visible = key_doc[k] == doc_q[d, :, cols]
        if causal:
            key_row = lax.broadcasted_iota(jnp.int32, (ROWS, HALF), 0)
            query_row = lax.broadcasted_iota(jnp.int32, (ROWS, HALF), 1) + cols.start
            visible = visible & (key_row <= query_row)
        scores = jnp.where(visible, scores, MASKED)
        old = stat[d, h, 0:1, cols]
        top = jnp.maximum(jnp.max(scores, axis=0, keepdims=True), old)
        weights = jnp.exp2((scores - top) * SCALE2)
        product = jnp.dot(
            vt_all[k, h], weights.astype(jnp.bfloat16), preferred_element_type=jnp.float32
        )
        fade = jnp.exp2((old - top) * SCALE2)
        total = stat[d, h, 1:2, cols] * fade + jnp.sum(weights, axis=0, keepdims=True)
        stat[d, h, 1:2, cols] = total
        stat[d, h, 0:1, cols] = top
        acc[d, h, :, cols] = acc[d, h, :, cols] * fade + product

    def tile(h, k, d, causal=False):
        for start in range(0, ROWS, HALF):
            half_tile(h, k, d, slice(start, start + HALF), causal)

    def give_back(h, d):
        o_send[h, d - 1] = acc[d, h].astype(jnp.bfloat16)
        o_copies[h][d - 1].start()
        s_copies[h][d - 1].start()

    acc[...] = jnp.zeros_like(acc)
    stat[:, :, 0:1] = jnp.full((NY, HEADS, 1, ROWS), MASKED, jnp.float32)
    stat[:, :, 1:2] = jnp.zeros((NY, HEADS, 1, ROWS), jnp.float32)
    key_doc[0] = turned_docs(doc_q[0])
    def own_tiles():
        for h in range(HEADS):
            tile(h, 0, 0, causal=True)

    @pl.when(z < REACH)
    def _():
        own_tiles()

    pl.semaphore_wait(barrier, len(partners))

    for k in range(1, REACH + 1):
        @pl.when(z + k < NZ)
        def _(k=k):
            dz_copies[k - 1].start()
    for copy in dy_copies + w1_copies:
        copy.start()
    for h in range(HEADS):
        for part in range(2):
            @pl.when(z < NZ - 1)
            def _(h=h, part=part):
                kv_copy(h, 0, part).start()
    for copy in q_copies:
        copy.start()
    for h, part in AROUND:
        @pl.when(sends_around)
        def _(h=h, part=part):
            around_out(h, part).start()

    @pl.when(z >= REACH)
    def _():
        own_tiles()

    advance(0, 1, 0)
    advance(0, 1, 1)
    for k in range(1, REACH + 1):
        @pl.when(z >= k)
        def _(k=k):
            dz_copies[k - 1].wait_recv()
            key_doc[k] = turned_docs(doc_k[k - 1])
    weight_over_y()
    advance(1, 1, 0)
    advance(1, 1, 1)
    for d in range(1, NY):
        q_copies[d - 1].wait_recv()
        dy_copies[d - 1].wait_recv()

    for h, part in AROUND:
        relay_around(h, part)

    for low in range(NY - 1):
        @pl.when(y == low)
        def _(low=low):
            for d in range(low + 1, NY):
                for h in range(HEADS):
                    tile(h, 0, d)

    def row(k, carry):
        @pl.when(k > 1)
        def _():
            advance(1, k, 0)

        @pl.when(z >= k)
        def _():
            for d in range(NY):
                tile(0, k, d)

        @pl.when(k > 1)
        def _():
            advance(1, k, 1)

        @pl.when(k == 2)
        def _():
            weight_over_x()

        advance(0, k + 1, 0)

        @pl.when(z >= k)
        def _():
            for d in range(NY):
                tile(1, k, d)

        advance(0, k + 1, 1)

        @pl.when(k == 2)
        def _():
            weight_over_core(0)

        return carry

    lax.fori_loop(1, REACH, row, 0)

    for h in range(HEADS):
        for d in range(1, NY):
            @pl.when(y < d)
            def _(h=h, d=d):
                give_back(h, d)

    advance(1, REACH, 0)
    for h in range(HEADS):
        if h == 1:
            advance(1, REACH, 1)
        for high in range(1, NY):
            @pl.when((z >= REACH) & (y == high))
            def _(h=h, high=high):
                for d in range(1, high + 1):
                    tile(h, REACH, d)

        for d in range(NY - 1, 0, -1):
            @pl.when(y >= d)
            def _(h=h, d=d):
                give_back(h, d)

        @pl.when(z >= REACH)
        def _(h=h):
            tile(h, REACH, 0)

    for dy in range(1, NY):
        weight_over_core(dy)

    for h in range(HEADS):
        for d in range(1, NY):
            o_copies[h][d - 1].wait_recv()
            s_copies[h][d - 1].wait_recv()
        tops = [stat[0, h, 0:1]] + [stat_recv[h, d, 0:1] for d in range(NY - 1)]
        sums = [stat[0, h, 1:2]] + [stat_recv[h, d, 1:2] for d in range(NY - 1)]
        top = tops[0]
        for other in tops[1:]:
            top = jnp.maximum(top, other)
        shares = [jnp.exp2((one - top) * SCALE2) for one in tops]
        total = sums[0] * shares[0]
        value = acc[0, h] * shares[0]
        for d in range(1, NY):
            total = total + sums[d] * shares[d]
            value = value + o_recv[h, d - 1].astype(jnp.float32) * shares[d]
        lse_ref[h : h + 1] = top * SCALE + jnp.log(total)
        value = value / total
        att[:, h * HEAD_DIM : (h + 1) * HEAD_DIM] = value.T.astype(jnp.bfloat16)

    for copy in sum(w4_copies, []):
        copy.wait_recv()
    for h, part in [(h, part) for h in range(HEADS) for part in range(2)]:
        for k in range(REACH - 1 if (h, part) in AROUND else REACH):
            @pl.when((z >= k) & (z < NZ - 1))
            def _(h=h, k=k, part=part):
                kv_copy(h, k, part).wait_send()
    for h, part in AROUND:
        @pl.when(sends_around)
        def _(h=h, part=part):
            around_out(h, part).wait_send()

        @pl.when(relays_around)
        def _(h=h, part=part):
            around_in(h, part).wait_send()
    for copy in q_copies + dy_copies + w1_copies + w2_copies + sum(w3_copies + w4_copies, []):
        copy.wait_send()
    for k in range(1, REACH + 1):
        @pl.when(z + k < NZ)
        def _(k=k):
            dz_copies[k - 1].wait_send()
    for h in range(HEADS):
        for copy in o_copies[h] + s_copies[h]:
            copy.wait_send()


def project_kernel(att, w_all, lse_in, out_ref, lse_ref, stage, sems):
    lse_copy = pltpu.make_async_copy(lse_in, lse_ref, sems.at[NZ])
    lse_copy.start()
    attended = att[...]
    writes = []
    width = NY * 128
    for block in range(NZ):
        weight = jnp.concatenate(
            [w_all[c, :, block * 128 : (block + 1) * 128] for c in range(NY)], axis=1
        )
        cols = slice(block * width, (block + 1) * width)
        stage[:, cols] = jnp.dot(
            attended, weight, preferred_element_type=jnp.float32
        ).astype(jnp.bfloat16)
        write = pltpu.make_async_copy(stage.at[:, cols], out_ref.at[:, cols], sems.at[block])
        write.start()
        writes.append(write)
    for write in writes + [lse_copy]:
        write.wait()


def on_device(queries, keys, values, document_ids, output_weight):
    bf16, f32, i32 = jnp.bfloat16, jnp.float32, jnp.int32
    dma = pltpu.SemaphoreType.DMA
    anywhere = pl.BlockSpec(memory_space=pl.ANY)
    local = pl.BlockSpec(memory_space=pltpu.VMEM)
    attended, weight, lse = pl.pallas_call(
        attend_kernel,
        out_shape=(
            jax.ShapeDtypeStruct((ROWS, FEATURES), bf16),
            jax.ShapeDtypeStruct((NY, FEATURES, NZ * 128), bf16),
            jax.ShapeDtypeStruct((HEADS, ROWS), f32),
        ),
        in_specs=[pl.BlockSpec(memory_space=pltpu.HBM)] * 5,
        out_specs=(local, anywhere, local),
        scratch_shapes=[
            pltpu.VMEM((NY, ROWS, FEATURES), bf16),
            pltpu.VMEM((REACH + 1, HEADS, ROWS, HEAD_DIM), bf16),
            pltpu.VMEM((REACH + 1, HEADS, HEAD_DIM, ROWS), bf16),
            pltpu.VMEM((ROWS, FEATURES), bf16),
            pltpu.VMEM((NY, 1, ROWS), i32),
            pltpu.VMEM((REACH, 1, ROWS), i32),
            pltpu.VMEM((REACH + 1, ROWS, 128), i32),
            pltpu.VMEM((NY, HEADS, HEAD_DIM, ROWS), f32),
            pltpu.VMEM((NY, HEADS, 2, ROWS), f32),
            pltpu.VMEM((HEADS, NY - 1, HEAD_DIM, ROWS), bf16),
            pltpu.VMEM((HEADS, NY - 1, HEAD_DIM, ROWS), bf16),
            pltpu.VMEM((HEADS, NY - 1, 2, ROWS), f32),
            pltpu.VMEM((HEADS, ROWS, HEAD_DIM), bf16),
            pltpu.VMEM((HEADS, HEAD_DIM, ROWS), bf16),
            dma((6,)),
            dma((HEADS, REACH, 2)), dma((HEADS, REACH, 2)),
            dma((HEADS, 2)), dma((HEADS, 2)), dma((HEADS, 2)),
            dma((NY - 1,)), dma((NY - 1,)), dma((NY - 1,)), dma((NY - 1,)),
            dma((REACH,)), dma((REACH,)),
            dma((NZ - 1,)), dma((NZ - 1,)), dma((NY - 1,)), dma((NY - 1,)),
            dma((NY, NX - 1)), dma((NY, NX - 1)), dma((NY, NX)), dma((NY, NX)),
            dma((HEADS, NY - 1)), dma((HEADS, NY - 1)),
            dma((HEADS, NY - 1)), dma((HEADS, NY - 1)),
        ],
        compiler_params=pltpu.CompilerParams(
            collective_id=0, has_side_effects=True, vmem_limit_bytes=32 << 20
        ),
    )(*[
        pltpu.with_memory_space_constraint(one, pltpu.HBM)
        for one in (queries, keys, values, document_ids.reshape(1, ROWS), output_weight)
    ])
    return pl.pallas_call(
        project_kernel,
        out_shape=(
            jax.ShapeDtypeStruct((ROWS, MODEL), bf16),
            jax.ShapeDtypeStruct((HEADS, ROWS), f32),
        ),
        in_specs=[local, local, anywhere],
        out_specs=(anywhere, anywhere),
        scratch_shapes=[pltpu.VMEM((ROWS, MODEL), bf16), dma((NZ + 1,))],
        compiler_params=pltpu.CompilerParams(vmem_limit_bytes=32 << 20),
    )(attended, weight, lse)


def solution(mesh):
    in_specs = (
        P(("dp", "ctx"), None),
        P(("dp", "ctx"), None),
        P(("dp", "ctx"), None),
        P(("dp", "ctx")),
        P(None, "ctx"),
    )
    out_specs = (P(("dp", "ctx"), None), P(None, ("dp", "ctx")))
    return jax.shard_map(
        on_device, mesh=mesh, in_specs=in_specs, out_specs=out_specs, check_vma=False
    )
```

```python
import math

import jax
import jax.numpy as jnp
from jax import lax
from jax.experimental import pallas as pl
from jax.experimental.pallas import tpu as pltpu
from jax.sharding import PartitionSpec as P

MESH = pl.DeviceIdType.MESH
HEADS = 2
HEAD_DIM = 128
NX, NC, NZ, NY = 4, 2, 8, 4
ROWS = 256
HALF = 128
FEATURES = HEADS * HEAD_DIM
MODEL = 4096
PARTS = NX * NC
PIECE = FEATURES // PARTS
REACH = 4
MASKED = -1e30
SCALE = 1.0 / math.sqrt(HEAD_DIM)
SCALE2 = SCALE * math.log2(math.e)
AROUND = [(0, 0), (0, 1)]
JUMP = 2


def attend_kernel(
    q_in, k_in, v_in, doc_in, w_in,
    att, w_all, lse_ref,
    q_all, k_all, vt_all, v_own, doc_q, doc_k, key_doc,
    acc, stat, o_send, o_recv, relay_k, relay_v,
    loc_sem, kv_ss, kv_rs, one_ss, one_rs, o_ss, o_rs,
):
    dp = lax.axis_index("dp")
    ctx = lax.axis_index("ctx")
    x, core = dp // NC, lax.rem(dp, NC)
    z, y = ctx // NY, lax.rem(ctx, NY)

    def at(dx=0, flip=False, dz=0, dy=0):
        x_to = lax.rem(x + dx + NX, NX)
        core_to = 1 - core if flip else core
        z_to = lax.rem(z + dz + NZ, NZ)
        y_to = lax.rem(y + dy + NY, NY)
        return (x_to * NC + core_to, z_to * NY + y_to)

    def remote(src, dst, ss, rs, to):
        return pltpu.make_async_remote_copy(
            src_ref=src, dst_ref=dst, send_sem=ss, recv_sem=rs, device_id=to, device_id_type=MESH
        )

    barrier = pltpu.get_barrier_semaphore()
    partners = [at(dz=d) for d in range(1, NZ)]
    partners += [at(dy=d) for d in range(1, NY)]
    partners += [at(dx=d) for d in range(1, NX)]
    partners += [at(flip=True)]
    for to in partners:
        pl.semaphore_signal(barrier, inc=1, device_id=to, device_id_type=MESH)

    piece = pl.ds(pl.multiple_of(dp * PIECE, PIECE), PIECE)
    z_cols = pl.ds(pl.multiple_of(z * 128, 128), 128)
    locals_ = [
        pltpu.make_async_copy(k_in.at[:, 0:128], k_all.at[0, 0], loc_sem.at[0]),
        pltpu.make_async_copy(k_in.at[:, 128:256], k_all.at[0, 1], loc_sem.at[1]),
        pltpu.make_async_copy(doc_in, doc_q.at[0], loc_sem.at[2]),
        pltpu.make_async_copy(w_in.at[piece], w_all.at[0, piece, z_cols], loc_sem.at[3]),
        pltpu.make_async_copy(v_in, v_own, loc_sem.at[4]),
        pltpu.make_async_copy(q_in, q_all.at[0], loc_sem.at[5]),
    ]
    for copy in locals_:
        copy.start()

    def wait_bytes(like, sem):
        pltpu.make_async_copy(like, like, sem).wait()

    def kv_copy(h, k, part):
        ref = (k_all, vt_all)[part]
        return remote(
            ref.at[k, h], ref.at[k + 1, h],
            kv_ss.at[k], kv_rs.at[h, k, part], at(dz=1),
        )

    def advance(h, k, part):
        @pl.when(z >= k)
        def _():
            kv_copy(h, k - 1, part).wait_recv()

        last = REACH - 2 if (h, part) in AROUND else REACH - 1

        @pl.when((z >= k) & (z < NZ - 1) & (k <= last))
        def _():
            kv_copy(h, k, part).start()

    def around_out(h, part):
        return remote(
            (k_all, vt_all)[part].at[0, h], (relay_k, relay_v)[part].at[h],
            one_ss.at[0], one_rs.at[0], at(dz=-JUMP),
        )

    def around_in(h, part):
        return remote(
            (relay_k, relay_v)[part].at[h], (k_all, vt_all)[part].at[REACH, h],
            one_ss.at[1], kv_rs.at[h, REACH - 1, part], at(dz=-JUMP),
        )

    sends_around = z < NZ - REACH
    relays_around = (z < NZ - REACH - JUMP) | (z >= NZ - JUMP)

    def relay_around():
        @pl.when(relays_around)
        def _():
            wait_bytes(k_all.at[0], one_rs.at[0])
            for h, part in AROUND:
                around_in(h, part).start()

    def group(index, pairs):
        return [remote(src, dst, one_ss.at[index], one_rs.at[index], to) for src, dst, to in pairs]

    q_copies = group(1 + 1, [(q_in, q_all.at[d], at(dy=d)) for d in range(1, NY)])
    dy_copies = group(3, [(doc_in, doc_q.at[d], at(dy=d)) for d in range(1, NY)])
    dz_copies = group(4, [(doc_in, doc_k.at[k - 1], at(dz=k)) for k in range(1, REACH + 1)])
    own_piece = w_all.at[0, piece, z_cols]
    w1_copies = group(5, [(own_piece, own_piece, at(dz=d)) for d in range(1, NZ)])
    own_column = w_all.at[0, piece]
    w2_copies = group(6, [(own_column, w_all.at[d, piece], at(dy=d)) for d in range(1, NY)])
    w3_first = group(7, [(own_column, own_column, at(dx=d)) for d in range(1, NX)])
    others = w_all.at[1:NY, piece]
    w3_rest = group(8, [(others, others, at(dx=d)) for d in range(1, NX)])

    def part_rows(dx):
        part = lax.rem(x - dx + NX, NX) * NC + core
        return w_all.at[:, pl.ds(pl.multiple_of(part * PIECE, PIECE), PIECE)]

    w4_copies = group(9, [(part_rows(d), part_rows(d), at(flip=True)) for d in range(NX)])

    def weight_over_y():
        wait_bytes(w_all.at[0, 0 : (NZ - 1) * PIECE, 0:128], one_rs.at[5])
        for copy in w2_copies + w3_first:
            copy.start()

    def weight_over_x():
        wait_bytes(w_all.at[1:NY, piece], one_rs.at[6])
        for copy in w3_rest:
            copy.start()
        w4_copies[0].start()

    def weight_over_core():
        wait_bytes(w_all.at[1:NY, piece], one_rs.at[7])
        wait_bytes(w_all.at[1:NY, 0 : (NX - 1) * PIECE], one_rs.at[8])
        for d in range(1, NX):
            w4_copies[d].start()

    o_copies = [
        [
            remote(o_send.at[h, d - 1], o_recv.at[h, d - 1], o_ss.at[h], o_rs.at[h], at(dy=-d))
            for d in range(1, NY)
        ]
        for h in range(HEADS)
    ]

    def turned_docs(row):
        return jnp.broadcast_to(row, (128, ROWS)).T

    def half_tile(h, k, d, cols, causal):
        scores = lax.dot_general(
            k_all[k, h], q_all[d, cols, h * HEAD_DIM : (h + 1) * HEAD_DIM],
            (((1,), (1,)), ((), ())), preferred_element_type=jnp.float32,
        )
        visible = key_doc[k] == doc_q[d, :, cols]
        if causal:
            key_row = lax.broadcasted_iota(jnp.int32, (ROWS, HALF), 0)
            query_row = lax.broadcasted_iota(jnp.int32, (ROWS, HALF), 1) + cols.start
            visible = visible & (key_row <= query_row)
        scores = jnp.where(visible, scores, MASKED)
        old = stat[d, h, 0:1, cols]
        top = jnp.maximum(jnp.max(scores, axis=0, keepdims=True), old)
        weights = jnp.exp2((scores - top) * SCALE2)
        product = jnp.dot(
            vt_all[k, h], weights.astype(jnp.bfloat16), preferred_element_type=jnp.float32
        )
        fade = jnp.exp2((old - top) * SCALE2)
        total = stat[d, h, 1:2, cols] * fade + jnp.sum(weights, axis=0, keepdims=True)
        stat[d, h, 1:2, cols] = total
        stat[d, h, 0:1, cols] = top
        acc[d, h, :, cols] = acc[d, h, :, cols] * fade + product

    def tile(h, k, d, causal=False):
        for start in range(0, ROWS, HALF):
            half_tile(h, k, d, slice(start, start + HALF), causal)

    def thirds(row):
        high = row.astype(jnp.bfloat16).astype(jnp.float32)
        rest = row - high
        middle = rest.astype(jnp.bfloat16).astype(jnp.float32)
        return [high, middle, rest - middle]

    def give_back(h, d):
        rows = thirds(stat[d, h, 0:1]) + thirds(stat[d, h, 1:2])
        rows += [jnp.zeros((16 - len(rows), ROWS), jnp.float32)]
        o_send[h, d - 1, 0:HEAD_DIM] = acc[d, h].astype(jnp.bfloat16)
        o_send[h, d - 1, HEAD_DIM : HEAD_DIM + 16] = jnp.concatenate(rows, axis=0).astype(jnp.bfloat16)
        o_copies[h][d - 1].start()

    locals_[0].wait()
    locals_[1].wait()
    pl.semaphore_wait(barrier, len(partners))

    def send_own(part):
        for h in range(HEADS):
            @pl.when(z < NZ - 1)
            def _(h=h):
                kv_copy(h, 0, part).start()

    send_own(0)
    for copy in dz_copies + dy_copies:
        copy.start()
    locals_[3].wait()
    for copy in w1_copies:
        copy.start()
    locals_[4].wait()
    v_turned = v_own[...].T
    for h in range(HEADS):
        vt_all[0, h] = v_turned[h * HEAD_DIM : (h + 1) * HEAD_DIM]
    send_own(1)
    for copy in q_copies:
        copy.start()
    for h, part in AROUND:
        @pl.when(sends_around)
        def _(h=h, part=part):
            around_out(h, part).start()

    locals_[2].wait()
    locals_[5].wait()
    acc[...] = jnp.zeros_like(acc)
    stat[:, :, 0:1] = jnp.full((NY, HEADS, 1, ROWS), MASKED, jnp.float32)
    stat[:, :, 1:2] = jnp.zeros((NY, HEADS, 1, ROWS), jnp.float32)
    key_doc[0] = turned_docs(doc_q[0])
    for h in range(HEADS):
        tile(h, 0, 0, causal=True)

    advance(0, 1, 0)
    advance(1, 1, 0)
    advance(0, 1, 1)
    wait_bytes(doc_k, one_rs.at[4])
    for k in range(1, REACH + 1):
        @pl.when(z >= k)
        def _(k=k):
            key_doc[k] = turned_docs(doc_k[k - 1])
    weight_over_y()
    advance(1, 1, 1)
    relay_around()
    wait_bytes(q_all.at[1:NY], one_rs.at[2])
    wait_bytes(doc_q.at[1:NY], one_rs.at[3])

    for low in range(NY - 1):
        @pl.when(y == low)
        def _(low=low):
            for d in range(low + 1, NY):
                for h in range(HEADS):
                    tile(h, 0, d)

    def give_back_early(h):
        for d in range(NY - 1, 0, -1):
            @pl.when(y < d)
            def _(d=d):
                give_back(h, d)

    def row(k, carry):
        @pl.when(k > 1)
        def _():
            advance(1, k, 0)

        @pl.when(z >= k)
        def _():
            for d in range(NY):
                tile(0, k, d)

        @pl.when(k > 1)
        def _():
            advance(1, k, 1)

        @pl.when(k == 1)
        def _():
            weight_over_x()

        @pl.when(k == REACH - 1)
        def _():
            give_back_early(0)

        advance(0, k + 1, 0)

        @pl.when(z >= k)
        def _():
            for d in range(NY):
                tile(1, k, d)

        advance(0, k + 1, 1)

        return carry

    lax.fori_loop(1, REACH, row, 0)

    for h in range(HEADS):
        if h == 1:
            give_back_early(1)
            advance(1, REACH, 0)
            advance(1, REACH, 1)
        for high in range(1, NY):
            @pl.when((z >= REACH) & (y == high))
            def _(h=h, high=high):
                for d in range(1, high + 1):
                    tile(h, REACH, d)

        for d in range(NY - 1, 0, -1):
            @pl.when(y >= d)
            def _(h=h, d=d):
                give_back(h, d)

        @pl.when(z >= REACH)
        def _(h=h):
            tile(h, REACH, 0)

    weight_over_core()

    for h in range(HEADS):
        wait_bytes(o_recv.at[h], o_rs.at[h])
        tops, sums = [stat[0, h, 0:1]], [stat[0, h, 1:2]]
        for d in range(NY - 1):
            rows = o_recv[h, d, HEAD_DIM : HEAD_DIM + 16].astype(jnp.float32)
            tops.append(rows[0:1] + rows[1:2] + rows[2:3])
            sums.append(rows[3:4] + rows[4:5] + rows[5:6])
        top = tops[0]
        for other in tops[1:]:
            top = jnp.maximum(top, other)
        shares = [jnp.exp2((one - top) * SCALE2) for one in tops]
        total = sums[0] * shares[0]
        value = acc[0, h] * shares[0]
        for d in range(1, NY):
            total = total + sums[d] * shares[d]
            value = value + o_recv[h, d - 1, 0:HEAD_DIM].astype(jnp.float32) * shares[d]
        lse_ref[h : h + 1] = top * SCALE + jnp.log(total)
        value = value / total
        att[:, h * HEAD_DIM : (h + 1) * HEAD_DIM] = value.T.astype(jnp.bfloat16)

    wait_bytes(w_all.at[:, 0 : NX * PIECE], one_rs.at[9])

    for k in range(REACH):
        @pl.when((z >= k) & (z < NZ - 1))
        def _(k=k):
            wait_bytes(k_all.at[0:2] if k < REACH - 1 else k_all.at[0], kv_ss.at[k])

    @pl.when(sends_around)
    def _():
        wait_bytes(k_all.at[0], one_ss.at[0])

    @pl.when(relays_around)
    def _():
        wait_bytes(k_all.at[0], one_ss.at[1])

    wait_bytes(q_all.at[1:NY], one_ss.at[2])
    wait_bytes(doc_q.at[1:NY], one_ss.at[3])
    wait_bytes(doc_k, one_ss.at[4])
    wait_bytes(w_all.at[0, 0 : (NZ - 1) * PIECE, 0:128], one_ss.at[5])
    wait_bytes(w_all.at[1:NY, piece], one_ss.at[6])
    wait_bytes(w_all.at[1:NY, piece], one_ss.at[7])
    wait_bytes(w_all.at[1:NY, 0 : (NX - 1) * PIECE], one_ss.at[8])
    wait_bytes(w_all.at[:, 0 : NX * PIECE], one_ss.at[9])
    for h in range(HEADS):
        wait_bytes(o_send.at[h], o_ss.at[h])


def project_kernel(att, w_all, lse_in, out_ref, lse_ref, stage, sems):
    lse_copy = pltpu.make_async_copy(lse_in, lse_ref, sems.at[NZ])
    lse_copy.start()
    attended = att[...]
    y = lax.rem(lax.axis_index("ctx"), NY)
    writes = []
    width = NY * 128
    for block in range(NZ):
        weight = jnp.concatenate(
            [w_all[lax.rem(y - c + NY, NY), :, block * 128 : (block + 1) * 128] for c in range(NY)], axis=1
        )
        cols = slice(block * width, (block + 1) * width)
        stage[:, cols] = jnp.dot(
            attended, weight, preferred_element_type=jnp.float32
        ).astype(jnp.bfloat16)
        write = pltpu.make_async_copy(stage.at[:, cols], out_ref.at[:, cols], sems.at[block])
        write.start()
        writes.append(write)
    for write in writes + [lse_copy]:
        write.wait()


def on_device(queries, keys, values, document_ids, output_weight):
    bf16, f32, i32 = jnp.bfloat16, jnp.float32, jnp.int32
    dma = pltpu.SemaphoreType.DMA
    anywhere = pl.BlockSpec(memory_space=pl.ANY)
    local = pl.BlockSpec(memory_space=pltpu.VMEM)
    attended, weight, lse = pl.pallas_call(
        attend_kernel,
        out_shape=(
            jax.ShapeDtypeStruct((ROWS, FEATURES), bf16),
            jax.ShapeDtypeStruct((NY, FEATURES, NZ * 128), bf16),
            jax.ShapeDtypeStruct((HEADS, ROWS), f32),
        ),
        in_specs=[pl.BlockSpec(memory_space=pltpu.HBM)] * 5,
        out_specs=(local, anywhere, local),
        scratch_shapes=[
            pltpu.VMEM((NY, ROWS, FEATURES), bf16),
            pltpu.VMEM((REACH + 1, HEADS, ROWS, HEAD_DIM), bf16),
            pltpu.VMEM((REACH + 1, HEADS, HEAD_DIM, ROWS), bf16),
            pltpu.VMEM((ROWS, FEATURES), bf16),
            pltpu.VMEM((NY, 1, ROWS), i32),
            pltpu.VMEM((REACH, 1, ROWS), i32),
            pltpu.VMEM((REACH + 1, ROWS, 128), i32),
            pltpu.VMEM((NY, HEADS, HEAD_DIM, ROWS), f32),
            pltpu.VMEM((NY, HEADS, 2, ROWS), f32),
            pltpu.VMEM((HEADS, NY - 1, HEAD_DIM + 16, ROWS), bf16),
            pltpu.VMEM((HEADS, NY - 1, HEAD_DIM + 16, ROWS), bf16),
            pltpu.VMEM((HEADS, ROWS, HEAD_DIM), bf16),
            pltpu.VMEM((HEADS, HEAD_DIM, ROWS), bf16),
            dma((6,)), dma((REACH,)), dma((HEADS, REACH, 2)),
            dma((10,)), dma((10,)), dma((HEADS,)), dma((HEADS,)),
        ],
        compiler_params=pltpu.CompilerParams(
            collective_id=0, has_side_effects=True, vmem_limit_bytes=32 << 20
        ),
    )(*[
        pltpu.with_memory_space_constraint(one, pltpu.HBM)
        for one in (queries, keys, values, document_ids.reshape(1, ROWS), output_weight)
    ])
    return pl.pallas_call(
        project_kernel,
        out_shape=(
            jax.ShapeDtypeStruct((ROWS, MODEL), bf16),
            jax.ShapeDtypeStruct((HEADS, ROWS), f32),
        ),
        in_specs=[local, local, anywhere],
        out_specs=(anywhere, anywhere),
        scratch_shapes=[pltpu.VMEM((ROWS, MODEL), bf16), dma((NZ + 1,))],
        compiler_params=pltpu.CompilerParams(vmem_limit_bytes=32 << 20),
    )(attended, weight, lse)


def solution(mesh):
    in_specs = (
        P(("dp", "ctx"), None),
        P(("dp", "ctx"), None),
        P(("dp", "ctx"), None),
        P(("dp", "ctx")),
        P(None, "ctx"),
    )
    out_specs = (P(("dp", "ctx"), None), P(None, ("dp", "ctx")))
    return jax.shard_map(
        on_device, mesh=mesh, in_specs=in_specs, out_specs=out_specs, check_vma=False
    )
```

```python
import math

import jax
import jax.numpy as jnp
from jax import lax
from jax.experimental import pallas as pl
from jax.experimental.pallas import tpu as pltpu
from jax.sharding import PartitionSpec as P

MESH = pl.DeviceIdType.MESH
HEADS = 2
HEAD_DIM = 128
NX, NC, NZ, NY = 4, 2, 8, 4
ROWS = 256
HALF = 128
FEATURES = HEADS * HEAD_DIM
MODEL = 4096
PARTS = NX * NC
PIECE = FEATURES // PARTS
REACH = 4
MASKED = -1e30
SCALE = 1.0 / math.sqrt(HEAD_DIM)
SCALE2 = SCALE * math.log2(math.e)
AROUND = [(0, 0), (0, 1), (1, 0)]
JUMP = 2


def attend_kernel(
    q_in, k_in, v_in, doc_in, w_in,
    att, w_all, lse_ref,
    q_all, k_all, vt_all, v_own, doc_q, doc_k, key_doc,
    acc, stat, o_send, o_recv, relay_k, relay_v, kept, kept_fade,
    loc_sem, kv_ss, kv_rs, a_ss, a_rs, one_ss, one_rs, o_ss, o_rs,
):
    dp = lax.axis_index("dp")
    ctx = lax.axis_index("ctx")
    x, core = dp // NC, lax.rem(dp, NC)
    z, y = ctx // NY, lax.rem(ctx, NY)

    def at(dx=0, flip=False, dz=0, dy=0):
        x_to = lax.rem(x + dx + NX, NX)
        core_to = 1 - core if flip else core
        z_to = lax.rem(z + dz + NZ, NZ)
        y_to = lax.rem(y + dy + NY, NY)
        return (x_to * NC + core_to, z_to * NY + y_to)

    def remote(src, dst, ss, rs, to):
        return pltpu.make_async_remote_copy(
            src_ref=src, dst_ref=dst, send_sem=ss, recv_sem=rs, device_id=to, device_id_type=MESH
        )

    barrier = pltpu.get_barrier_semaphore()
    partners = [at(dz=d) for d in range(1, NZ)]
    partners += [at(dy=d) for d in range(1, NY)]
    partners += [at(dx=d) for d in range(1, NX)]
    partners += [at(flip=True)]
    for to in partners:
        pl.semaphore_signal(barrier, inc=1, device_id=to, device_id_type=MESH)

    piece = pl.ds(pl.multiple_of(dp * PIECE, PIECE), PIECE)
    z_cols = pl.ds(pl.multiple_of(z * 128, 128), 128)
    locals_ = [
        pltpu.make_async_copy(k_in.at[:, 0:128], k_all.at[0, 0], loc_sem.at[0]),
        pltpu.make_async_copy(k_in.at[:, 128:256], k_all.at[0, 1], loc_sem.at[1]),
        pltpu.make_async_copy(doc_in, doc_q.at[0], loc_sem.at[2]),
        pltpu.make_async_copy(w_in.at[piece], w_all.at[0, piece, z_cols], loc_sem.at[3]),
        pltpu.make_async_copy(v_in, v_own, loc_sem.at[4]),
        pltpu.make_async_copy(q_in, q_all.at[0], loc_sem.at[5]),
    ]
    for copy in locals_:
        copy.start()

    def wait_bytes(like, sem):
        pltpu.make_async_copy(like, like, sem).wait()

    def kv_copy(h, k, part):
        ref = (k_all, vt_all)[part]
        return remote(
            ref.at[k, h], ref.at[k + 1, h],
            kv_ss.at[k], kv_rs.at[h, k, part], at(dz=1),
        )

    def advance(h, k, part):
        @pl.when(z >= k)
        def _():
            kv_copy(h, k - 1, part).wait_recv()

        last = REACH - 2 if (h, part) in AROUND else REACH - 1

        @pl.when((z >= k) & (z < NZ - 1) & (k <= last))
        def _():
            kv_copy(h, k, part).start()

    def around_out(h, part):
        return remote(
            (k_all, vt_all)[part].at[0, h], (relay_k, relay_v)[part].at[h],
            a_ss.at[0], a_rs.at[AROUND.index((h, part))], at(dz=-JUMP),
        )

    def around_in(h, part):
        return remote(
            (relay_k, relay_v)[part].at[h], (k_all, vt_all)[part].at[REACH, h],
            a_ss.at[1], kv_rs.at[h, REACH - 1, part], at(dz=-JUMP),
        )

    sends_around = z < NZ - REACH

    def send_around(index):
        @pl.when(sends_around)
        def _():
            around_out(*AROUND[index]).start()

    def relay_around(index, here):
        @pl.when(here)
        def _():
            around_out(*AROUND[index]).wait_recv()
            around_in(*AROUND[index]).start()

    relays_low = (z < NZ - REACH - JUMP) | (z == NZ - 1)
    relays_high = (z >= NZ - JUMP) & (z < NZ - 1)

    def group(index, pairs):
        return [remote(src, dst, one_ss.at[index], one_rs.at[index], to) for src, dst, to in pairs]

    q_copies = group(1 + 1, [(q_in, q_all.at[d], at(dy=d)) for d in range(1, NY)])
    dy_copies = group(3, [(doc_in, doc_q.at[d], at(dy=d)) for d in range(1, NY)])
    dz_copies = group(4, [(doc_in, doc_k.at[k - 1], at(dz=k)) for k in range(1, REACH + 1)])
    own_piece = w_all.at[0, piece, z_cols]
    w1_copies = group(5, [(own_piece, own_piece, at(dz=d)) for d in range(1, NZ)])
    own_column = w_all.at[0, piece]
    w2_copies = group(6, [(own_column, w_all.at[d, piece], at(dy=d)) for d in range(1, NY)])
    w3_first = group(7, [(own_column, own_column, at(dx=d)) for d in range(1, NX)])
    others = w_all.at[1:NY, piece]
    w3_rest = group(8, [(others, others, at(dx=d)) for d in (1, NX - 1)])
    far_part = lax.rem(x + NX // 2, NX) * NC + core
    far_rows = pl.ds(pl.multiple_of(far_part * PIECE, PIECE), PIECE)
    w2_far = group(0, [(w_all.at[0, far_rows], w_all.at[d, far_rows], at(dy=d)) for d in range(1, NY)])

    def part_rows(dx):
        part = lax.rem(x - dx + NX, NX) * NC + core
        return w_all.at[:, pl.ds(pl.multiple_of(part * PIECE, PIECE), PIECE)]

    w4_copies = group(9, [(part_rows(d), part_rows(d), at(flip=True)) for d in range(NX)])

    def weight_over_y():
        wait_bytes(w_all.at[0, 0 : (NZ - 1) * PIECE, 0:128], one_rs.at[5])
        for copy in w2_copies + w3_first:
            copy.start()

    def weight_over_x():
        wait_bytes(w_all.at[1:NY, piece], one_rs.at[6])
        for copy in w3_rest:
            copy.start()
        wait_bytes(w_all.at[1:NY, piece], one_rs.at[7])
        for copy in w2_far:
            copy.start()
        w4_copies[0].start()

    def weight_over_core():
        wait_bytes(w_all.at[1:NY, 0 : 2 * PIECE], one_rs.at[8])
        wait_bytes(w_all.at[1:NY, piece], one_rs.at[0])
        for d in range(1, NX):
            w4_copies[d].start()

    o_copies = [
        [
            remote(o_send.at[h, d - 1], o_recv.at[h, d - 1], o_ss.at[h], o_rs.at[h], at(dy=-d))
            for d in range(1, NY)
        ]
        for h in range(HEADS)
    ]

    def turned_docs(row):
        return jnp.broadcast_to(row, (128, ROWS)).T

    def half_weights(h, k, d, cols, causal):
        head = pl.ds(h * HEAD_DIM if isinstance(h, int) else pl.multiple_of(h * HEAD_DIM, HEAD_DIM), HEAD_DIM)
        scores = lax.dot_general(
            k_all[k, h], q_all[d, cols, head],
            (((1,), (1,)), ((), ())), preferred_element_type=jnp.float32,
        )
        visible = key_doc[k] == doc_q[d, :, cols]
        if causal:
            key_row = lax.broadcasted_iota(jnp.int32, (ROWS, HALF), 0)
            query_row = lax.broadcasted_iota(jnp.int32, (ROWS, HALF), 1) + cols.start
            visible = visible & (key_row <= query_row)
        scores = jnp.where(visible, scores, MASKED)
        old = stat[d, h, 0:1, cols]
        top = jnp.maximum(jnp.max(scores, axis=0, keepdims=True), old)
        weights = jnp.exp2((scores - top) * SCALE2)
        fade = jnp.exp2((old - top) * SCALE2)
        total = stat[d, h, 1:2, cols] * fade + jnp.sum(weights, axis=0, keepdims=True)
        stat[d, h, 1:2, cols] = total
        stat[d, h, 0:1, cols] = top
        return weights.astype(jnp.bfloat16), fade

    def half_sum(h, k, d, cols, weights, fade):
        product = jnp.dot(vt_all[k, h], weights, preferred_element_type=jnp.float32)
        acc[d, h, :, cols] = acc[d, h, :, cols] * fade + product

    halves = [slice(start, start + HALF) for start in range(0, ROWS, HALF)]

    def tile(h, k, d, causal=False):
        for cols in halves:
            half_sum(h, k, d, cols, *half_weights(h, k, d, cols, causal))

    def tile_weights(h, k, d):
        for cols in halves:
            kept[d, :, cols], kept_fade[d, 0:1, cols] = half_weights(h, k, d, cols, False)

    def tile_sum(h, k, d):
        for cols in halves:
            half_sum(h, k, d, cols, kept[d, :, cols], kept_fade[d, 0:1, cols])

    def thirds(row):
        high = row.astype(jnp.bfloat16).astype(jnp.float32)
        rest = row - high
        middle = rest.astype(jnp.bfloat16).astype(jnp.float32)
        return [high, middle, rest - middle]

    def give_back(h, d):
        rows = thirds(stat[d, h, 0:1]) + thirds(stat[d, h, 1:2])
        rows += [jnp.zeros((16 - len(rows), ROWS), jnp.float32)]
        o_send[h, d - 1, 0:HEAD_DIM] = acc[d, h].astype(jnp.bfloat16)
        o_send[h, d - 1, HEAD_DIM : HEAD_DIM + 16] = jnp.concatenate(rows, axis=0).astype(jnp.bfloat16)
        o_copies[h][d - 1].start()

    locals_[0].wait()
    locals_[1].wait()
    pl.semaphore_wait(barrier, len(partners))

    def send_own(h, part):
        @pl.when(z < NZ - 1)
        def _():
            kv_copy(h, 0, part).start()

    send_own(0, 0)
    send_around(0)
    for copy in dz_copies + dy_copies:
        copy.start()
    locals_[3].wait()
    locals_[4].wait()
    v_turned = v_own[...].T
    for h in range(HEADS):
        vt_all[0, h] = v_turned[h * HEAD_DIM : (h + 1) * HEAD_DIM]
    send_own(0, 1)
    for copy in q_copies:
        copy.start()
    send_own(1, 1)
    for copy in w1_copies:
        copy.start()
    send_around(1)

    locals_[2].wait()
    locals_[5].wait()
    acc[...] = jnp.zeros_like(acc)
    stat[:, :, 0:1] = jnp.full((NY, HEADS, 1, ROWS), MASKED, jnp.float32)
    stat[:, :, 1:2] = jnp.zeros((NY, HEADS, 1, ROWS), jnp.float32)
    key_doc[0] = turned_docs(doc_q[0])
    for h in range(HEADS):
        tile(h, 0, 0, causal=True)

    advance(0, 1, 0)
    advance(0, 1, 1)
    send_own(1, 0)
    send_around(2)
    wait_bytes(doc_k, one_rs.at[4])
    for k in range(1, REACH + 1):
        @pl.when(z >= k)
        def _(k=k):
            key_doc[k] = turned_docs(doc_k[k - 1])
    weight_over_y()
    relay_around(0, relays_low)
    advance(0, 2, 0)
    advance(1, 1, 1)
    relay_around(1, relays_low)
    wait_bytes(q_all.at[1:NY], one_rs.at[2])
    wait_bytes(doc_q.at[1:NY], one_rs.at[3])

    for low in range(NY - 1):
        @pl.when(y == low)
        def _(low=low):
            for d in range(low + 1, NY):
                for h in range(HEADS):
                    tile(h, 0, d)

    def give_back_early(h):
        for d in range(NY - 1, 0, -1):
            @pl.when(y < d)
            def _(d=d):
                give_back(h, d)

    def far(h, step):
        for high in range(1, NY):
            @pl.when((z >= REACH) & (y == high))
            def _(high=high):
                for d in range(1, high + 1):
                    step(h, REACH, d)

    def give_back_late(h):
        for d in range(NY - 1, 0, -1):
            @pl.when(y >= d)
            def _(d=d):
                give_back(h, d)

    def far_own(h):
        @pl.when(z >= REACH)
        def _():
            tile(h, REACH, 0)

    arrivals = [
        [(0, 2, 1), (1, 1, 0)],
        [],
        [(1, 2, 1)],
        [(0, 3, 0), (0, 3, 1)],
        [(1, 2, 0)],
        [(1, 3, 1)],
    ]

    def unit(u, carry):
        for index, chunks in enumerate(arrivals):
            @pl.when(u == index)
            def _(index=index, chunks=chunks):
                if index == 2:
                    weight_over_x()
                    for chunk in range(len(AROUND)):
                        relay_around(chunk, relays_high)
                for chunk in chunks:
                    advance(*chunk)
                if index == 0:
                    relay_around(2, relays_low)
                if index == 4:
                    give_back_early(0)
                if index == 5:
                    advance(0, REACH, 0)
                    advance(0, REACH, 1)
                    far(0, tile)
                    give_back_late(0)
                    advance(1, 3, 0)

        past = [0, (u + 4) // 5, (u + 3) // 5, u // 3, u // 4, u // 5]
        h = past[2] - past[3] + past[4]
        k = 1 + past[1] - past[2] + 2 * past[3] - past[4] + past[5]

        @pl.when(z >= k)
        def _():
            for d in range(NY):
                tile(h, k, d)

        return carry

    lax.fori_loop(0, len(arrivals), unit, 0)
    give_back_early(1)

    advance(1, REACH, 0)
    far(1, tile_weights)
    advance(1, REACH, 1)
    for d in range(NY - 1, 0, -1):
        @pl.when((z >= REACH) & (y >= d))
        def _(d=d):
            tile_sum(1, REACH, d)

        @pl.when(y >= d)
        def _(d=d):
            give_back(1, d)
    far_own(0)
    far_own(1)
    weight_over_core()

    for h in range(HEADS):
        wait_bytes(o_recv.at[h], o_rs.at[h])
        tops, sums = [stat[0, h, 0:1]], [stat[0, h, 1:2]]
        for d in range(NY - 1):
            rows = o_recv[h, d, HEAD_DIM : HEAD_DIM + 16].astype(jnp.float32)
            tops.append(rows[0:1] + rows[1:2] + rows[2:3])
            sums.append(rows[3:4] + rows[4:5] + rows[5:6])
        top = tops[0]
        for other in tops[1:]:
            top = jnp.maximum(top, other)
        shares = [jnp.exp2((one - top) * SCALE2) for one in tops]
        total = sums[0] * shares[0]
        for d in range(1, NY):
            total = total + sums[d] * shares[d]
        lse_ref[h : h + 1] = top * SCALE + jnp.log(total)
        value = acc[0, h] * (shares[0] / total)
        for d in range(1, NY):
            value = value + o_recv[h, d - 1, 0:HEAD_DIM].astype(jnp.float32) * (shares[d] / total)
        att[:, h * HEAD_DIM : (h + 1) * HEAD_DIM] = value.T.astype(jnp.bfloat16)

    wait_bytes(w_all.at[:, 0 : NX * PIECE], one_rs.at[9])

    for k in range(REACH):
        @pl.when((z >= k) & (z < NZ - 1))
        def _(k=k):
            wait_bytes(k_all.at[0:2] if k < REACH - 1 else k_all.at[0, 0], kv_ss.at[k])

    @pl.when(sends_around)
    def _():
        wait_bytes(k_all.at[0:3, 0], a_ss.at[0])

    @pl.when(relays_low | relays_high)
    def _():
        wait_bytes(k_all.at[0:3, 0], a_ss.at[1])

    wait_bytes(q_all.at[1:NY], one_ss.at[2])
    wait_bytes(doc_q.at[1:NY], one_ss.at[3])
    wait_bytes(doc_k, one_ss.at[4])
    wait_bytes(w_all.at[0, 0 : (NZ - 1) * PIECE, 0:128], one_ss.at[5])
    wait_bytes(w_all.at[1:NY, piece], one_ss.at[6])
    wait_bytes(w_all.at[1:NY, piece], one_ss.at[7])
    wait_bytes(w_all.at[1:NY, 0 : 2 * PIECE], one_ss.at[8])
    wait_bytes(w_all.at[1:NY, piece], one_ss.at[0])
    wait_bytes(w_all.at[:, 0 : NX * PIECE], one_ss.at[9])
    for h in range(HEADS):
        wait_bytes(o_send.at[h], o_ss.at[h])


def project_kernel(att, w_all, lse_in, out_ref, lse_ref, stage, sems):
    lse_copy = pltpu.make_async_copy(lse_in, lse_ref, sems.at[NZ])
    lse_copy.start()
    attended = att[...]
    y = lax.rem(lax.axis_index("ctx"), NY)
    writes = []
    width = NY * 128
    for block in range(NZ):
        weight = jnp.concatenate(
            [w_all[lax.rem(y - c + NY, NY), :, block * 128 : (block + 1) * 128] for c in range(NY)], axis=1
        )
        cols = slice(block * width, (block + 1) * width)
        stage[:, cols] = jnp.dot(
            attended, weight, preferred_element_type=jnp.float32
        ).astype(jnp.bfloat16)
        write = pltpu.make_async_copy(stage.at[:, cols], out_ref.at[:, cols], sems.at[block])
        write.start()
        writes.append(write)
    for write in writes + [lse_copy]:
        write.wait()


def on_device(queries, keys, values, document_ids, output_weight):
    bf16, f32, i32 = jnp.bfloat16, jnp.float32, jnp.int32
    dma = pltpu.SemaphoreType.DMA
    anywhere = pl.BlockSpec(memory_space=pl.ANY)
    local = pl.BlockSpec(memory_space=pltpu.VMEM)
    attended, weight, lse = pl.pallas_call(
        attend_kernel,
        out_shape=(
            jax.ShapeDtypeStruct((ROWS, FEATURES), bf16),
            jax.ShapeDtypeStruct((NY, FEATURES, NZ * 128), bf16),
            jax.ShapeDtypeStruct((HEADS, ROWS), f32),
        ),
        in_specs=[pl.BlockSpec(memory_space=pltpu.HBM)] * 5,
        out_specs=(local, anywhere, local),
        scratch_shapes=[
            pltpu.VMEM((NY, ROWS, FEATURES), bf16),
            pltpu.VMEM((REACH + 1, HEADS, ROWS, HEAD_DIM), bf16),
            pltpu.VMEM((REACH + 1, HEADS, HEAD_DIM, ROWS), bf16),
            pltpu.VMEM((ROWS, FEATURES), bf16),
            pltpu.VMEM((NY, 1, ROWS), i32),
            pltpu.VMEM((REACH, 1, ROWS), i32),
            pltpu.VMEM((REACH + 1, ROWS, 128), i32),
            pltpu.VMEM((NY, HEADS, HEAD_DIM, ROWS), f32),
            pltpu.VMEM((NY, HEADS, 2, ROWS), f32),
            pltpu.VMEM((HEADS, NY - 1, HEAD_DIM + 16, ROWS), bf16),
            pltpu.VMEM((HEADS, NY - 1, HEAD_DIM + 16, ROWS), bf16),
            pltpu.VMEM((HEADS, ROWS, HEAD_DIM), bf16),
            pltpu.VMEM((HEADS, HEAD_DIM, ROWS), bf16),
            pltpu.VMEM((NY, ROWS, ROWS), bf16),
            pltpu.VMEM((NY, 1, ROWS), f32),
            dma((6,)), dma((REACH,)), dma((HEADS, REACH, 2)), dma((2,)), dma((3,)),
            dma((10,)), dma((10,)), dma((HEADS,)), dma((HEADS,)),
        ],
        compiler_params=pltpu.CompilerParams(
            collective_id=0, has_side_effects=True, vmem_limit_bytes=32 << 20
        ),
    )(*[
        pltpu.with_memory_space_constraint(one, pltpu.HBM)
        for one in (queries, keys, values, document_ids.reshape(1, ROWS), output_weight)
    ])
    return pl.pallas_call(
        project_kernel,
        out_shape=(
            jax.ShapeDtypeStruct((ROWS, MODEL), bf16),
            jax.ShapeDtypeStruct((HEADS, ROWS), f32),
        ),
        in_specs=[local, local, anywhere],
        out_specs=(anywhere, anywhere),
        scratch_shapes=[pltpu.VMEM((ROWS, MODEL), bf16), dma((NZ + 1,))],
        compiler_params=pltpu.CompilerParams(vmem_limit_bytes=32 << 20),
    )(attended, weight, lse)


def solution(mesh):
    in_specs = (
        P(("dp", "ctx"), None),
        P(("dp", "ctx"), None),
        P(("dp", "ctx"), None),
        P(("dp", "ctx")),
        P(None, "ctx"),
    )
    out_specs = (P(("dp", "ctx"), None), P(None, ("dp", "ctx")))
    return jax.shard_map(
        on_device, mesh=mesh, in_specs=in_specs, out_specs=out_specs, check_vma=False
    )
```

```python
import math

import jax
import jax.numpy as jnp
from jax import lax
from jax.experimental import pallas as pl
from jax.experimental.pallas import tpu as pltpu
from jax.sharding import PartitionSpec as P

MESH = pl.DeviceIdType.MESH
HEADS = 2
HEAD_DIM = 128
NX, NC, NZ, NY = 4, 2, 8, 4
ROWS = 256
HALF = 128
FEATURES = HEADS * HEAD_DIM
MODEL = 4096
PARTS = NX * NC
PIECE = FEATURES // PARTS
REACH = 4
MASKED = -1e30
SCALE = 1.0 / math.sqrt(HEAD_DIM)
SCALE2 = SCALE * math.log2(math.e)
AROUND = [(0, 0), (0, 1), (1, 0)]
JUMP = 2


def attend_kernel(
    q_in, k_in, v_in, doc_in, w_in,
    att, w_all, lse_ref,
    q_all, k_all, vt_all, v_own, doc_q, doc_k, key_doc,
    acc, stat, o_send, o_recv, relay_k, relay_v, kept, kept_fade,
    loc_sem, kv_ss, kv_rs, a_ss, a_rs, one_ss, one_rs, o_ss, o_rs,
):
    dp = lax.axis_index("dp")
    ctx = lax.axis_index("ctx")
    x, core = dp // NC, lax.rem(dp, NC)
    z, y = ctx // NY, lax.rem(ctx, NY)

    def at(dx=0, flip=False, dz=0, dy=0):
        x_to = lax.rem(x + dx + NX, NX)
        core_to = 1 - core if flip else core
        z_to = lax.rem(z + dz + NZ, NZ)
        y_to = lax.rem(y + dy + NY, NY)
        return (x_to * NC + core_to, z_to * NY + y_to)

    def remote(src, dst, ss, rs, to):
        return pltpu.make_async_remote_copy(
            src_ref=src, dst_ref=dst, send_sem=ss, recv_sem=rs, device_id=to, device_id_type=MESH
        )

    barrier = pltpu.get_barrier_semaphore()
    partners = [at(dz=d) for d in range(1, NZ)]
    partners += [at(dy=d) for d in range(1, NY)]
    partners += [at(dx=d) for d in range(1, NX)]
    partners += [at(flip=True)]
    for to in partners:
        pl.semaphore_signal(barrier, inc=1, device_id=to, device_id_type=MESH)

    piece = pl.ds(pl.multiple_of(dp * PIECE, PIECE), PIECE)
    z_cols = pl.ds(pl.multiple_of(z * 128, 128), 128)
    locals_ = [
        pltpu.make_async_copy(k_in.at[:, 0:128], k_all.at[0, 0], loc_sem.at[0]),
        pltpu.make_async_copy(k_in.at[:, 128:256], k_all.at[0, 1], loc_sem.at[1]),
        pltpu.make_async_copy(doc_in, doc_q.at[0], loc_sem.at[2]),
        pltpu.make_async_copy(w_in.at[piece], w_all.at[0, piece, z_cols], loc_sem.at[3]),
        pltpu.make_async_copy(v_in, v_own, loc_sem.at[4]),
        pltpu.make_async_copy(q_in, q_all.at[0], loc_sem.at[5]),
    ]
    for copy in locals_:
        copy.start()

    def wait_bytes(like, sem):
        pltpu.make_async_copy(like, like, sem).wait()

    def kv_copy(h, k, part):
        ref = (k_all, vt_all)[part]
        return remote(
            ref.at[k, h], ref.at[k + 1, h],
            kv_ss.at[k], kv_rs.at[h, k, part], at(dz=1),
        )

    def advance(h, k, part):
        @pl.when(z >= k)
        def _():
            kv_copy(h, k - 1, part).wait_recv()

        last = REACH - 2 if (h, part) in AROUND else REACH - 1

        @pl.when((z >= k) & (z < NZ - 1) & (k <= last))
        def _():
            kv_copy(h, k, part).start()

    def around_out(h, part):
        return remote(
            (k_all, vt_all)[part].at[0, h], (relay_k, relay_v)[part].at[h],
            a_ss.at[0], a_rs.at[AROUND.index((h, part))], at(dz=-JUMP),
        )

    def around_in(h, part):
        return remote(
            (relay_k, relay_v)[part].at[h], (k_all, vt_all)[part].at[REACH, h],
            a_ss.at[1], kv_rs.at[h, REACH - 1, part], at(dz=-JUMP),
        )

    sends_around = z < NZ - REACH

    def send_around(index):
        @pl.when(sends_around)
        def _():
            around_out(*AROUND[index]).start()

    def relay_around(index, here):
        @pl.when(here)
        def _():
            around_out(*AROUND[index]).wait_recv()
            around_in(*AROUND[index]).start()

    relays_low = (z < NZ - REACH - JUMP) | (z == NZ - 1)
    relays_high = (z >= NZ - JUMP) & (z < NZ - 1)

    def group(index, pairs):
        return [remote(src, dst, one_ss.at[index], one_rs.at[index], to) for src, dst, to in pairs]

    q_copies = group(1 + 1, [(q_in, q_all.at[d], at(dy=d)) for d in range(1, NY)])
    dy_copies = group(3, [(doc_in, doc_q.at[d], at(dy=d)) for d in range(1, NY)])
    dz_copies = group(4, [(doc_in, doc_k.at[k - 1], at(dz=k)) for k in range(1, REACH + 1)])
    own_piece = w_all.at[0, piece, z_cols]
    w1_copies = group(5, [(own_piece, own_piece, at(dz=d)) for d in range(1, NZ)])
    own_column = w_all.at[0, piece]
    w2_copies = group(6, [(own_column, w_all.at[d, piece], at(dy=d)) for d in range(1, NY)])
    w3_first = group(7, [(own_column, own_column, at(dx=d)) for d in range(1, NX)])
    others = w_all.at[1:NY, piece]
    w3_rest = group(8, [(others, others, at(dx=d)) for d in (1, NX - 1)])
    far_part = lax.rem(x + NX // 2, NX) * NC + core
    far_rows = pl.ds(pl.multiple_of(far_part * PIECE, PIECE), PIECE)
    w2_far = group(0, [(w_all.at[0, far_rows], w_all.at[d, far_rows], at(dy=d)) for d in range(1, NY)])

    def part_rows(dx):
        part = lax.rem(x - dx + NX, NX) * NC + core
        return w_all.at[:, pl.ds(pl.multiple_of(part * PIECE, PIECE), PIECE)]

    w4_copies = group(9, [(part_rows(d), part_rows(d), at(flip=True)) for d in range(NX)])

    def weight_over_y():
        wait_bytes(w_all.at[0, 0 : (NZ - 1) * PIECE, 0:128], one_rs.at[5])
        for copy in w2_copies + w3_first:
            copy.start()

    def weight_over_x():
        wait_bytes(w_all.at[1:NY, piece], one_rs.at[6])
        for copy in w3_rest:
            copy.start()
        wait_bytes(w_all.at[1:NY, piece], one_rs.at[7])
        for copy in w2_far:
            copy.start()
        w4_copies[0].start()

    def weight_over_core():
        wait_bytes(w_all.at[1:NY, 0 : 2 * PIECE], one_rs.at[8])
        wait_bytes(w_all.at[1:NY, piece], one_rs.at[0])
        for d in range(1, NX):
            w4_copies[d].start()

    o_copies = [
        [
            remote(o_send.at[h, d - 1], o_recv.at[h, d - 1], o_ss.at[h], o_rs.at[h], at(dy=-d))
            for d in range(1, NY)
        ]
        for h in range(HEADS)
    ]

    def turned_docs(row):
        return jnp.broadcast_to(row, (128, ROWS)).T

    def half_weights(h, k, d, cols, causal):
        head = pl.ds(h * HEAD_DIM if isinstance(h, int) else pl.multiple_of(h * HEAD_DIM, HEAD_DIM), HEAD_DIM)
        scores = lax.dot_general(
            k_all[k, h], q_all[d, cols, head],
            (((1,), (1,)), ((), ())), preferred_element_type=jnp.float32,
        )
        visible = key_doc[k] == doc_q[d, :, cols]
        if causal:
            key_row = lax.broadcasted_iota(jnp.int32, (ROWS, HALF), 0)
            query_row = lax.broadcasted_iota(jnp.int32, (ROWS, HALF), 1) + cols.start
            visible = visible & (key_row <= query_row)
        scores = jnp.where(visible, scores, MASKED)
        old = stat[d, h, 0:1, cols]
        top = jnp.maximum(jnp.max(scores, axis=0, keepdims=True), old)
        weights = jnp.exp2((scores - top) * SCALE2)
        fade = jnp.exp2((old - top) * SCALE2)
        total = stat[d, h, 1:2, cols] * fade + jnp.sum(weights, axis=0, keepdims=True)
        stat[d, h, 1:2, cols] = total
        stat[d, h, 0:1, cols] = top
        return weights.astype(jnp.bfloat16), fade

    def half_sum(h, k, d, cols, weights, fade):
        product = jnp.dot(vt_all[k, h], weights, preferred_element_type=jnp.float32)
        acc[d, h, :, cols] = acc[d, h, :, cols] * fade + product

    halves = [slice(start, start + HALF) for start in range(0, ROWS, HALF)]

    def tile(h, k, d, causal=False):
        for cols in halves:
            half_sum(h, k, d, cols, *half_weights(h, k, d, cols, causal))

    def tile_weights(h, k, d):
        for cols in halves:
            kept[d, :, cols], kept_fade[d, 0:1, cols] = half_weights(h, k, d, cols, False)

    def tile_sum(h, k, d):
        for cols in halves:
            half_sum(h, k, d, cols, kept[d, :, cols], kept_fade[d, 0:1, cols])

    def thirds(row):
        high = row.astype(jnp.bfloat16).astype(jnp.float32)
        rest = row - high
        middle = rest.astype(jnp.bfloat16).astype(jnp.float32)
        return [high, middle, rest - middle]

    def give_back(h, d):
        rows = thirds(stat[d, h, 0:1]) + thirds(stat[d, h, 1:2])
        rows += [jnp.zeros((16 - len(rows), ROWS), jnp.float32)]
        o_send[h, d - 1, 0:HEAD_DIM] = acc[d, h].astype(jnp.bfloat16)
        o_send[h, d - 1, HEAD_DIM : HEAD_DIM + 16] = jnp.concatenate(rows, axis=0).astype(jnp.bfloat16)
        o_copies[h][d - 1].start()

    locals_[0].wait()
    locals_[1].wait()
    pl.semaphore_wait(barrier, len(partners))

    def send_own(h, part):
        @pl.when(z < NZ - 1)
        def _():
            kv_copy(h, 0, part).start()

    send_own(0, 0)
    send_around(0)
    for copy in dz_copies + dy_copies:
        copy.start()
    locals_[3].wait()
    locals_[4].wait()
    v_turned = v_own[...].T
    for h in range(HEADS):
        vt_all[0, h] = v_turned[h * HEAD_DIM : (h + 1) * HEAD_DIM]
    send_own(0, 1)
    for copy in q_copies:
        copy.start()
    send_own(1, 1)
    for copy in w1_copies:
        copy.start()
    send_around(1)

    locals_[2].wait()
    locals_[5].wait()
    acc[...] = jnp.zeros_like(acc)
    stat[:, :, 0:1] = jnp.full((NY, HEADS, 1, ROWS), MASKED, jnp.float32)
    stat[:, :, 1:2] = jnp.zeros((NY, HEADS, 1, ROWS), jnp.float32)
    key_doc[0] = turned_docs(doc_q[0])
    for h in range(HEADS):
        tile(h, 0, 0, causal=True)

    advance(0, 1, 0)
    advance(0, 1, 1)
    send_own(1, 0)
    send_around(2)
    wait_bytes(doc_k, one_rs.at[4])
    for k in range(1, REACH + 1):
        @pl.when(z >= k)
        def _(k=k):
            key_doc[k] = turned_docs(doc_k[k - 1])
    relay_around(0, relays_low)
    advance(0, 2, 0)
    advance(1, 1, 1)
    weight_over_y()
    relay_around(1, relays_low)
    wait_bytes(q_all.at[1:NY], one_rs.at[2])
    wait_bytes(doc_q.at[1:NY], one_rs.at[3])

    for low in range(NY - 1):
        @pl.when(y == low)
        def _(low=low):
            for d in range(low + 1, NY):
                for h in range(HEADS):
                    tile(h, 0, d)

    def give_back_early(h):
        for d in range(NY - 1, 0, -1):
            @pl.when(y < d)
            def _(d=d):
                give_back(h, d)

    def far(h, step):
        for high in range(1, NY):
            @pl.when((z >= REACH) & (y == high))
            def _(high=high):
                for d in range(1, high + 1):
                    step(h, REACH, d)

    def give_back_late(h):
        for d in range(NY - 1, 0, -1):
            @pl.when(y >= d)
            def _(d=d):
                give_back(h, d)

    def far_own(h):
        @pl.when(z >= REACH)
        def _():
            tile(h, REACH, 0)

    arrivals = [
        [(0, 2, 1), (1, 1, 0)],
        [],
        [(1, 2, 1)],
        [(0, 3, 0), (0, 3, 1)],
        [(1, 2, 0)],
    ]

    def unit(u, carry):
        for index, chunks in enumerate(arrivals):
            @pl.when(u == index)
            def _(index=index, chunks=chunks):
                if index == 2:
                    weight_over_x()
                    for chunk in range(len(AROUND)):
                        relay_around(chunk, relays_high)
                for chunk in chunks:
                    advance(*chunk)
                if index == 0:
                    relay_around(2, relays_low)
                if index == 4:
                    give_back_early(0)

        past = [0, (u + 4) // 5, (u + 3) // 5, u // 3, u // 4, u // 5]
        h = past[2] - past[3] + past[4]
        k = 1 + past[1] - past[2] + 2 * past[3] - past[4] + past[5]

        @pl.when(z >= k)
        def _():
            for d in range(NY):
                tile(h, k, d)

        return carry

    lax.fori_loop(0, len(arrivals), unit, 0)
    advance(1, 3, 1)
    advance(0, REACH, 0)
    advance(0, REACH, 1)
    far(0, tile)
    give_back_late(0)
    advance(1, 3, 0)

    def near_last(first):
        for high in range(NY):
            @pl.when((z >= REACH - 1) & (y == high))
            def _(high=high):
                for d in range(1, high + 1) if first else [0, *range(high + 1, NY)]:
                    tile(1, REACH - 1, d)

    near_last(True)

    advance(1, REACH, 0)
    far(1, tile_weights)
    advance(1, REACH, 1)
    for d in range(NY - 1, 0, -1):
        @pl.when((z >= REACH) & (y >= d))
        def _(d=d):
            tile_sum(1, REACH, d)

        @pl.when(y >= d)
        def _(d=d):
            give_back(1, d)
    near_last(False)
    give_back_early(1)
    far_own(0)
    far_own(1)
    weight_over_core()

    for h in range(HEADS):
        wait_bytes(o_recv.at[h], o_rs.at[h])
        tops, sums = [stat[0, h, 0:1]], [stat[0, h, 1:2]]
        for d in range(NY - 1):
            rows = o_recv[h, d, HEAD_DIM : HEAD_DIM + 16].astype(jnp.float32)
            tops.append(rows[0:1] + rows[1:2] + rows[2:3])
            sums.append(rows[3:4] + rows[4:5] + rows[5:6])
        top = tops[0]
        for other in tops[1:]:
            top = jnp.maximum(top, other)
        shares = [jnp.exp2((one - top) * SCALE2) for one in tops]
        total = sums[0] * shares[0]
        for d in range(1, NY):
            total = total + sums[d] * shares[d]
        lse_ref[h : h + 1] = top * SCALE + jnp.log(total)
        value = acc[0, h] * (shares[0] / total)
        for d in range(1, NY):
            value = value + o_recv[h, d - 1, 0:HEAD_DIM].astype(jnp.float32) * (shares[d] / total)
        att[:, h * HEAD_DIM : (h + 1) * HEAD_DIM] = value.T.astype(jnp.bfloat16)

    wait_bytes(w_all.at[:, 0 : NX * PIECE], one_rs.at[9])

    for k in range(REACH):
        @pl.when((z >= k) & (z < NZ - 1))
        def _(k=k):
            wait_bytes(k_all.at[0:2] if k < REACH - 1 else k_all.at[0, 0], kv_ss.at[k])

    @pl.when(sends_around)
    def _():
        wait_bytes(k_all.at[0:3, 0], a_ss.at[0])

    @pl.when(relays_low | relays_high)
    def _():
        wait_bytes(k_all.at[0:3, 0], a_ss.at[1])

    wait_bytes(q_all.at[1:NY], one_ss.at[2])
    wait_bytes(doc_q.at[1:NY], one_ss.at[3])
    wait_bytes(doc_k, one_ss.at[4])
    wait_bytes(w_all.at[0, 0 : (NZ - 1) * PIECE, 0:128], one_ss.at[5])
    wait_bytes(w_all.at[1:NY, piece], one_ss.at[6])
    wait_bytes(w_all.at[1:NY, piece], one_ss.at[7])
    wait_bytes(w_all.at[1:NY, 0 : 2 * PIECE], one_ss.at[8])
    wait_bytes(w_all.at[1:NY, piece], one_ss.at[0])
    wait_bytes(w_all.at[:, 0 : NX * PIECE], one_ss.at[9])
    for h in range(HEADS):
        wait_bytes(o_send.at[h], o_ss.at[h])


def project_kernel(att, w_all, lse_in, out_ref, lse_ref, stage, sems):
    lse_copy = pltpu.make_async_copy(lse_in, lse_ref, sems.at[NZ])
    lse_copy.start()
    attended = att[...]
    y = lax.rem(lax.axis_index("ctx"), NY)
    writes = []
    width = NY * 128
    for block in range(NZ):
        weight = jnp.concatenate(
            [w_all[lax.rem(y - c + NY, NY), :, block * 128 : (block + 1) * 128] for c in range(NY)], axis=1
        )
        cols = slice(block * width, (block + 1) * width)
        stage[:, cols] = jnp.dot(
            attended, weight, preferred_element_type=jnp.float32
        ).astype(jnp.bfloat16)
        write = pltpu.make_async_copy(stage.at[:, cols], out_ref.at[:, cols], sems.at[block])
        write.start()
        writes.append(write)
    for write in writes + [lse_copy]:
        write.wait()


def on_device(queries, keys, values, document_ids, output_weight):
    bf16, f32, i32 = jnp.bfloat16, jnp.float32, jnp.int32
    dma = pltpu.SemaphoreType.DMA
    anywhere = pl.BlockSpec(memory_space=pl.ANY)
    local = pl.BlockSpec(memory_space=pltpu.VMEM)
    attended, weight, lse = pl.pallas_call(
        attend_kernel,
        out_shape=(
            jax.ShapeDtypeStruct((ROWS, FEATURES), bf16),
            jax.ShapeDtypeStruct((NY, FEATURES, NZ * 128), bf16),
            jax.ShapeDtypeStruct((HEADS, ROWS), f32),
        ),
        in_specs=[pl.BlockSpec(memory_space=pltpu.HBM)] * 5,
        out_specs=(local, anywhere, local),
        scratch_shapes=[
            pltpu.VMEM((NY, ROWS, FEATURES), bf16),
            pltpu.VMEM((REACH + 1, HEADS, ROWS, HEAD_DIM), bf16),
            pltpu.VMEM((REACH + 1, HEADS, HEAD_DIM, ROWS), bf16),
            pltpu.VMEM((ROWS, FEATURES), bf16),
            pltpu.VMEM((NY, 1, ROWS), i32),
            pltpu.VMEM((REACH, 1, ROWS), i32),
            pltpu.VMEM((REACH + 1, ROWS, 128), i32),
            pltpu.VMEM((NY, HEADS, HEAD_DIM, ROWS), f32),
            pltpu.VMEM((NY, HEADS, 2, ROWS), f32),
            pltpu.VMEM((HEADS, NY - 1, HEAD_DIM + 16, ROWS), bf16),
            pltpu.VMEM((HEADS, NY - 1, HEAD_DIM + 16, ROWS), bf16),
            pltpu.VMEM((HEADS, ROWS, HEAD_DIM), bf16),
            pltpu.VMEM((HEADS, HEAD_DIM, ROWS), bf16),
            pltpu.VMEM((NY, ROWS, ROWS), bf16),
            pltpu.VMEM((NY, 1, ROWS), f32),
            dma((6,)), dma((REACH,)), dma((HEADS, REACH, 2)), dma((2,)), dma((3,)),
            dma((10,)), dma((10,)), dma((HEADS,)), dma((HEADS,)),
        ],
        compiler_params=pltpu.CompilerParams(
            collective_id=0, has_side_effects=True, vmem_limit_bytes=32 << 20
        ),
    )(*[
        pltpu.with_memory_space_constraint(one, pltpu.HBM)
        for one in (queries, keys, values, document_ids.reshape(1, ROWS), output_weight)
    ])
    return pl.pallas_call(
        project_kernel,
        out_shape=(
            jax.ShapeDtypeStruct((ROWS, MODEL), bf16),
            jax.ShapeDtypeStruct((HEADS, ROWS), f32),
        ),
        in_specs=[local, local, anywhere],
        out_specs=(anywhere, anywhere),
        scratch_shapes=[pltpu.VMEM((ROWS, MODEL), bf16), dma((NZ + 1,))],
        compiler_params=pltpu.CompilerParams(vmem_limit_bytes=32 << 20),
    )(attended, weight, lse)


def solution(mesh):
    in_specs = (
        P(("dp", "ctx"), None),
        P(("dp", "ctx"), None),
        P(("dp", "ctx"), None),
        P(("dp", "ctx")),
        P(None, "ctx"),
    )
    out_specs = (P(("dp", "ctx"), None), P(None, ("dp", "ctx")))
    return jax.shard_map(
        on_device, mesh=mesh, in_specs=in_specs, out_specs=out_specs, check_vma=False
    )
```

```python
import math

import jax
import jax.numpy as jnp
from jax import lax
from jax.experimental import pallas as pl
from jax.experimental.pallas import tpu as pltpu
from jax.sharding import PartitionSpec as P

MESH = pl.DeviceIdType.MESH
HEADS = 2
HEAD_DIM = 128
NX, NC, NZ, NY = 4, 2, 8, 4
ROWS = 256
HALF = 128
FEATURES = HEADS * HEAD_DIM
MODEL = 4096
PARTS = NX * NC
PIECE = FEATURES // PARTS
REACH = 4
MASKED = -1e30
SCALE = 1.0 / math.sqrt(HEAD_DIM)
SCALE2 = SCALE * math.log2(math.e)
AROUND = [(0, 0), (0, 1), (1, 0)]
JUMP = 2


def attend_kernel(
    q_in, k_in, v_in, doc_in, w_in,
    att, w_all, lse_ref,
    q_all, k_all, vt_all, v_own, doc_q, doc_k, key_doc,
    acc, stat, o_send, o_recv, relay_k, relay_v, kept, kept_fade,
    loc_sem, kv_ss, kv_rs, a_ss, a_rs, one_ss, one_rs, o_ss, o_rs,
):
    dp = lax.axis_index("dp")
    ctx = lax.axis_index("ctx")
    x, core = dp // NC, lax.rem(dp, NC)
    z, y = ctx // NY, lax.rem(ctx, NY)

    def at(dx=0, flip=False, dz=0, dy=0):
        x_to = lax.rem(x + dx + NX, NX)
        core_to = 1 - core if flip else core
        z_to = lax.rem(z + dz + NZ, NZ)
        y_to = lax.rem(y + dy + NY, NY)
        return (x_to * NC + core_to, z_to * NY + y_to)

    def remote(src, dst, ss, rs, to):
        return pltpu.make_async_remote_copy(
            src_ref=src, dst_ref=dst, send_sem=ss, recv_sem=rs, device_id=to, device_id_type=MESH
        )

    barrier = pltpu.get_barrier_semaphore()
    partners = [at(dz=d) for d in range(1, NZ)]
    partners += [at(dy=d) for d in range(1, NY)]
    partners += [at(dx=d) for d in range(1, NX)]
    partners += [at(flip=True)]
    for to in partners:
        pl.semaphore_signal(barrier, inc=1, device_id=to, device_id_type=MESH)

    piece = pl.ds(pl.multiple_of(dp * PIECE, PIECE), PIECE)
    z_cols = pl.ds(pl.multiple_of(z * 128, 128), 128)
    locals_ = [
        pltpu.make_async_copy(k_in.at[:, 0:128], k_all.at[0, 0], loc_sem.at[0]),
        pltpu.make_async_copy(k_in.at[:, 128:256], k_all.at[0, 1], loc_sem.at[1]),
        pltpu.make_async_copy(doc_in, doc_q.at[0], loc_sem.at[2]),
        pltpu.make_async_copy(w_in.at[piece], w_all.at[0, piece, z_cols], loc_sem.at[3]),
        pltpu.make_async_copy(v_in, v_own, loc_sem.at[4]),
        pltpu.make_async_copy(q_in, q_all.at[0], loc_sem.at[5]),
    ]
    for copy in locals_:
        copy.start()

    def wait_bytes(like, sem):
        pltpu.make_async_copy(like, like, sem).wait()

    def kv_copy(h, k, part):
        ref = (k_all, vt_all)[part]
        return remote(
            ref.at[k, h], ref.at[k + 1, h],
            kv_ss.at[k], kv_rs.at[h, k, part], at(dz=1),
        )

    def advance(h, k, part):
        @pl.when(z >= k)
        def _():
            kv_copy(h, k - 1, part).wait_recv()

        last = REACH - 2 if (h, part) in AROUND else REACH - 1

        @pl.when((z >= k) & (z < NZ - 1) & (k <= last))
        def _():
            kv_copy(h, k, part).start()

    def around_out(h, part):
        return remote(
            (k_all, vt_all)[part].at[0, h], (relay_k, relay_v)[part].at[h],
            a_ss.at[0], a_rs.at[AROUND.index((h, part))], at(dz=-JUMP),
        )

    def around_in(h, part):
        return remote(
            (relay_k, relay_v)[part].at[h], (k_all, vt_all)[part].at[REACH, h],
            a_ss.at[1], kv_rs.at[h, REACH - 1, part], at(dz=-JUMP),
        )

    sends_around = z < NZ - REACH

    def send_around(index):
        @pl.when(sends_around)
        def _():
            around_out(*AROUND[index]).start()

    def relay_around(index, here):
        @pl.when(here)
        def _():
            around_out(*AROUND[index]).wait_recv()
            around_in(*AROUND[index]).start()

    relays_low = (z < NZ - REACH - JUMP) | (z == NZ - 1)
    relays_high = (z >= NZ - JUMP) & (z < NZ - 1)

    def group(index, pairs):
        return [remote(src, dst, one_ss.at[index], one_rs.at[index], to) for src, dst, to in pairs]

    q_copies = group(1 + 1, [(q_in, q_all.at[d], at(dy=d)) for d in range(1, NY)])
    dy_copies = group(3, [(doc_in, doc_q.at[d], at(dy=d)) for d in range(1, NY)])
    dz_copies = group(4, [(doc_in, doc_k.at[k - 1], at(dz=k)) for k in range(1, REACH + 1)])
    own_piece = w_all.at[0, piece, z_cols]
    w1_copies = group(5, [(own_piece, own_piece, at(dz=d)) for d in range(1, NZ)])
    own_column = w_all.at[0, piece]
    w2_copies = group(6, [(own_column, w_all.at[d, piece], at(dy=d)) for d in range(1, NY)])
    w3_first = group(7, [(own_column, own_column, at(dx=d)) for d in range(1, NX)])
    others = w_all.at[1:NY, piece]
    w3_rest = group(8, [(others, others, at(dx=d)) for d in (1, NX - 1)])
    far_part = lax.rem(x + NX // 2, NX) * NC + core
    far_rows = pl.ds(pl.multiple_of(far_part * PIECE, PIECE), PIECE)
    w2_far = group(0, [(w_all.at[0, far_rows], w_all.at[d, far_rows], at(dy=d)) for d in range(1, NY)])

    def part_rows(dx):
        part = lax.rem(x - dx + NX, NX) * NC + core
        return w_all.at[:, pl.ds(pl.multiple_of(part * PIECE, PIECE), PIECE)]

    w4_copies = group(9, [(part_rows(d), part_rows(d), at(flip=True)) for d in range(NX)])

    def weight_over_y():
        wait_bytes(w_all.at[0, 0 : (NZ - 1) * PIECE, 0:128], one_rs.at[5])
        for copy in w2_copies + w3_first:
            copy.start()

    def weight_over_x():
        wait_bytes(w_all.at[1:NY, piece], one_rs.at[6])
        for copy in w3_rest:
            copy.start()
        wait_bytes(w_all.at[1:NY, piece], one_rs.at[7])
        for copy in w2_far:
            copy.start()
        w4_copies[0].start()

    def weight_over_core():
        wait_bytes(w_all.at[1:NY, 0 : 2 * PIECE], one_rs.at[8])
        for d in (1, NX - 1):
            w4_copies[d].start()
        wait_bytes(w_all.at[1:NY, piece], one_rs.at[0])
        w4_copies[NX // 2].start()

    o_copies = [
        [
            remote(o_send.at[h, d - 1], o_recv.at[h, d - 1], o_ss.at[h], o_rs.at[h], at(dy=-d))
            for d in range(1, NY)
        ]
        for h in range(HEADS)
    ]

    def turned_docs(row):
        return jnp.broadcast_to(row, (128, ROWS)).T

    def half_weights(h, k, d, cols, causal):
        head = pl.ds(h * HEAD_DIM if isinstance(h, int) else pl.multiple_of(h * HEAD_DIM, HEAD_DIM), HEAD_DIM)
        scores = lax.dot_general(
            k_all[k, h], q_all[d, cols, head],
            (((1,), (1,)), ((), ())), preferred_element_type=jnp.float32,
        )
        visible = key_doc[k] == doc_q[d, :, cols]
        if causal:
            key_row = lax.broadcasted_iota(jnp.int32, (ROWS, HALF), 0)
            query_row = lax.broadcasted_iota(jnp.int32, (ROWS, HALF), 1) + cols.start
            visible = visible & (key_row <= query_row)
        scores = jnp.where(visible, scores, MASKED)
        old = stat[d, h, 0:1, cols]
        top = jnp.maximum(jnp.max(scores, axis=0, keepdims=True), old)
        weights = jnp.exp2((scores - top) * SCALE2)
        fade = jnp.exp2((old - top) * SCALE2)
        total = stat[d, h, 1:2, cols] * fade + jnp.sum(weights, axis=0, keepdims=True)
        stat[d, h, 1:2, cols] = total
        stat[d, h, 0:1, cols] = top
        return weights.astype(jnp.bfloat16), fade

    def half_sum(h, k, d, cols, weights, fade):
        product = jnp.dot(vt_all[k, h], weights, preferred_element_type=jnp.float32)
        acc[d, h, :, cols] = acc[d, h, :, cols] * fade + product

    halves = [slice(start, start + HALF) for start in range(0, ROWS, HALF)]

    def tile(h, k, d, causal=False):
        for cols in halves:
            half_sum(h, k, d, cols, *half_weights(h, k, d, cols, causal))

    def tile_weights(h, k, d):
        for cols in halves:
            kept[d, :, cols], kept_fade[d, 0:1, cols] = half_weights(h, k, d, cols, False)

    def tile_sum(h, k, d):
        for cols in halves:
            half_sum(h, k, d, cols, kept[d, :, cols], kept_fade[d, 0:1, cols])

    def thirds(row):
        high = row.astype(jnp.bfloat16).astype(jnp.float32)
        rest = row - high
        middle = rest.astype(jnp.bfloat16).astype(jnp.float32)
        return [high, middle, rest - middle]

    def give_back(h, d):
        rows = thirds(stat[d, h, 0:1]) + thirds(stat[d, h, 1:2])
        rows += [jnp.zeros((16 - len(rows), ROWS), jnp.float32)]
        o_send[h, d - 1, 0:HEAD_DIM] = acc[d, h].astype(jnp.bfloat16)
        o_send[h, d - 1, HEAD_DIM : HEAD_DIM + 16] = jnp.concatenate(rows, axis=0).astype(jnp.bfloat16)
        o_copies[h][d - 1].start()

    locals_[0].wait()
    locals_[1].wait()
    pl.semaphore_wait(barrier, len(partners))

    def send_own(h, part):
        @pl.when(z < NZ - 1)
        def _():
            kv_copy(h, 0, part).start()

    send_own(0, 0)
    send_around(0)
    for copy in dz_copies + dy_copies:
        copy.start()
    locals_[3].wait()
    locals_[4].wait()
    v_turned = v_own[...].T
    for h in range(HEADS):
        vt_all[0, h] = v_turned[h * HEAD_DIM : (h + 1) * HEAD_DIM]
    send_own(0, 1)
    for d in (2, 1, 3):
        q_copies[d - 1].start()
    send_own(1, 1)
    for copy in w1_copies:
        copy.start()
    send_around(1)

    locals_[2].wait()
    locals_[5].wait()
    acc[...] = jnp.zeros_like(acc)
    stat[:, :, 0:1] = jnp.full((NY, HEADS, 1, ROWS), MASKED, jnp.float32)
    stat[:, :, 1:2] = jnp.zeros((NY, HEADS, 1, ROWS), jnp.float32)
    key_doc[0] = turned_docs(doc_q[0])
    for h in range(HEADS):
        tile(h, 0, 0, causal=True)

    advance(0, 1, 0)
    advance(0, 1, 1)
    send_own(1, 0)
    send_around(2)
    wait_bytes(doc_k, one_rs.at[4])
    for k in range(1, REACH + 1):
        @pl.when(z >= k)
        def _(k=k):
            key_doc[k] = turned_docs(doc_k[k - 1])
    relay_around(0, relays_low)
    advance(0, 2, 0)
    advance(1, 1, 1)
    weight_over_y()
    relay_around(1, relays_low)
    wait_bytes(q_all.at[1:NY], one_rs.at[2])
    wait_bytes(doc_q.at[1:NY], one_rs.at[3])

    for low in range(NY - 1):
        @pl.when(y == low)
        def _(low=low):
            for d in range(low + 1, NY):
                for h in range(HEADS):
                    tile(h, 0, d)

    def give_back_early(h):
        for d in range(NY - 1, 0, -1):
            @pl.when(y < d)
            def _(d=d):
                give_back(h, d)

    def far(h, step):
        for high in range(1, NY):
            @pl.when((z >= REACH) & (y == high))
            def _(high=high):
                for d in range(1, high + 1):
                    step(h, REACH, d)

    def give_back_late(h):
        for d in range(NY - 1, 0, -1):
            @pl.when(y >= d)
            def _(d=d):
                give_back(h, d)

    def far_own(h):
        @pl.when(z >= REACH)
        def _():
            tile(h, REACH, 0)

    arrivals = [
        [(0, 2, 1), (1, 1, 0)],
        [],
        [(1, 2, 1)],
        [(0, 3, 0), (0, 3, 1)],
        [(1, 2, 0)],
    ]

    def unit(u, carry):
        for index, chunks in enumerate(arrivals):
            @pl.when(u == index)
            def _(index=index, chunks=chunks):
                if index == 2:
                    weight_over_x()
                    for chunk in range(len(AROUND)):
                        relay_around(chunk, relays_high)
                for chunk in chunks:
                    advance(*chunk)
                if index == 0:
                    relay_around(2, relays_low)
                if index == 4:
                    give_back_early(0)

        past = [0, (u + 4) // 5, (u + 3) // 5, u // 3, u // 4, u // 5]
        h = past[2] - past[3] + past[4]
        k = 1 + past[1] - past[2] + 2 * past[3] - past[4] + past[5]

        @pl.when(z >= k)
        def _():
            for d in range(NY):
                tile(h, k, d)

        return carry

    lax.fori_loop(0, len(arrivals), unit, 0)
    advance(1, 3, 1)
    advance(0, REACH, 0)
    advance(0, REACH, 1)
    far(0, tile)
    give_back_late(0)
    advance(1, 3, 0)

    def near_last(first):
        for high in range(NY):
            @pl.when((z >= REACH - 1) & (y == high))
            def _(high=high):
                for d in range(1, high + 1) if first else [0, *range(high + 1, NY)]:
                    tile(1, REACH - 1, d)

    near_last(True)

    advance(1, REACH, 0)
    far(1, tile_weights)
    advance(1, REACH, 1)
    for d in range(NY - 1, 0, -1):
        @pl.when((z >= REACH) & (y >= d))
        def _(d=d):
            tile_sum(1, REACH, d)

        @pl.when(y >= d)
        def _(d=d):
            give_back(1, d)
    near_last(False)
    give_back_early(1)
    far_own(0)
    far_own(1)
    weight_over_core()

    for h in range(HEADS):
        wait_bytes(o_recv.at[h], o_rs.at[h])
        tops, sums = [stat[0, h, 0:1]], [stat[0, h, 1:2]]
        for d in range(NY - 1):
            rows = o_recv[h, d, HEAD_DIM : HEAD_DIM + 16].astype(jnp.float32)
            tops.append(rows[0:1] + rows[1:2] + rows[2:3])
            sums.append(rows[3:4] + rows[4:5] + rows[5:6])
        top = tops[0]
        for other in tops[1:]:
            top = jnp.maximum(top, other)
        shares = [jnp.exp2((one - top) * SCALE2) for one in tops]
        total = sums[0] * shares[0]
        for d in range(1, NY):
            total = total + sums[d] * shares[d]
        lse_ref[h : h + 1] = top * SCALE + jnp.log(total)
        value = acc[0, h] * (shares[0] / total)
        for d in range(1, NY):
            value = value + o_recv[h, d - 1, 0:HEAD_DIM].astype(jnp.float32) * (shares[d] / total)
        att[:, h * HEAD_DIM : (h + 1) * HEAD_DIM] = value.astype(jnp.bfloat16).T

    wait_bytes(w_all.at[:, 0 : NX * PIECE], one_rs.at[9])

    for k in range(REACH):
        @pl.when((z >= k) & (z < NZ - 1))
        def _(k=k):
            wait_bytes(k_all.at[0:2] if k < REACH - 1 else k_all.at[0, 0], kv_ss.at[k])

    @pl.when(sends_around)
    def _():
        wait_bytes(k_all.at[0:3, 0], a_ss.at[0])

    @pl.when(relays_low | relays_high)
    def _():
        wait_bytes(k_all.at[0:3, 0], a_ss.at[1])

    wait_bytes(q_all.at[1:NY], one_ss.at[2])
    wait_bytes(doc_q.at[1:NY], one_ss.at[3])
    wait_bytes(doc_k, one_ss.at[4])
    wait_bytes(w_all.at[0, 0 : (NZ - 1) * PIECE, 0:128], one_ss.at[5])
    wait_bytes(w_all.at[1:NY, piece], one_ss.at[6])
    wait_bytes(w_all.at[1:NY, piece], one_ss.at[7])
    wait_bytes(w_all.at[1:NY, 0 : 2 * PIECE], one_ss.at[8])
    wait_bytes(w_all.at[1:NY, piece], one_ss.at[0])
    wait_bytes(w_all.at[:, 0 : NX * PIECE], one_ss.at[9])
    for h in range(HEADS):
        wait_bytes(o_send.at[h], o_ss.at[h])


def project_kernel(att, w_all, lse_in, out_ref, lse_ref, stage, sems):
    lse_copy = pltpu.make_async_copy(lse_in, lse_ref, sems.at[NZ])
    lse_copy.start()
    attended = att[...]
    y = lax.rem(lax.axis_index("ctx"), NY)
    writes = []
    width = NY * 128
    for block in range(NZ):
        weight = jnp.concatenate(
            [w_all[lax.rem(y - c + NY, NY), :, block * 128 : (block + 1) * 128] for c in range(NY)], axis=1
        )
        cols = slice(block * width, (block + 1) * width)
        stage[:, cols] = jnp.dot(
            attended, weight, preferred_element_type=jnp.float32
        ).astype(jnp.bfloat16)
        write = pltpu.make_async_copy(stage.at[:, cols], out_ref.at[:, cols], sems.at[block])
        write.start()
        writes.append(write)
    for write in writes + [lse_copy]:
        write.wait()


def on_device(queries, keys, values, document_ids, output_weight):
    bf16, f32, i32 = jnp.bfloat16, jnp.float32, jnp.int32
    dma = pltpu.SemaphoreType.DMA
    anywhere = pl.BlockSpec(memory_space=pl.ANY)
    local = pl.BlockSpec(memory_space=pltpu.VMEM)
    attended, weight, lse = pl.pallas_call(
        attend_kernel,
        out_shape=(
            jax.ShapeDtypeStruct((ROWS, FEATURES), bf16),
            jax.ShapeDtypeStruct((NY, FEATURES, NZ * 128), bf16),
            jax.ShapeDtypeStruct((HEADS, ROWS), f32),
        ),
        in_specs=[pl.BlockSpec(memory_space=pltpu.HBM)] * 5,
        out_specs=(local, anywhere, local),
        scratch_shapes=[
            pltpu.VMEM((NY, ROWS, FEATURES), bf16),
            pltpu.VMEM((REACH + 1, HEADS, ROWS, HEAD_DIM), bf16),
            pltpu.VMEM((REACH + 1, HEADS, HEAD_DIM, ROWS), bf16),
            pltpu.VMEM((ROWS, FEATURES), bf16),
            pltpu.VMEM((NY, 1, ROWS), i32),
            pltpu.VMEM((REACH, 1, ROWS), i32),
            pltpu.VMEM((REACH + 1, ROWS, 128), i32),
            pltpu.VMEM((NY, HEADS, HEAD_DIM, ROWS), f32),
            pltpu.VMEM((NY, HEADS, 2, ROWS), f32),
            pltpu.VMEM((HEADS, NY - 1, HEAD_DIM + 16, ROWS), bf16),
            pltpu.VMEM((HEADS, NY - 1, HEAD_DIM + 16, ROWS), bf16),
            pltpu.VMEM((HEADS, ROWS, HEAD_DIM), bf16),
            pltpu.VMEM((HEADS, HEAD_DIM, ROWS), bf16),
            pltpu.VMEM((NY, ROWS, ROWS), bf16),
            pltpu.VMEM((NY, 1, ROWS), f32),
            dma((6,)), dma((REACH,)), dma((HEADS, REACH, 2)), dma((2,)), dma((3,)),
            dma((10,)), dma((10,)), dma((HEADS,)), dma((HEADS,)),
        ],
        compiler_params=pltpu.CompilerParams(
            collective_id=0, has_side_effects=True, vmem_limit_bytes=32 << 20
        ),
    )(*[
        pltpu.with_memory_space_constraint(one, pltpu.HBM)
        for one in (queries, keys, values, document_ids.reshape(1, ROWS), output_weight)
    ])
    return pl.pallas_call(
        project_kernel,
        out_shape=(
            jax.ShapeDtypeStruct((ROWS, MODEL), bf16),
            jax.ShapeDtypeStruct((HEADS, ROWS), f32),
        ),
        in_specs=[local, local, anywhere],
        out_specs=(anywhere, anywhere),
        scratch_shapes=[pltpu.VMEM((ROWS, MODEL), bf16), dma((NZ + 1,))],
        compiler_params=pltpu.CompilerParams(vmem_limit_bytes=32 << 20),
    )(attended, weight, lse)


def solution(mesh):
    in_specs = (
        P(("dp", "ctx"), None),
        P(("dp", "ctx"), None),
        P(("dp", "ctx"), None),
        P(("dp", "ctx")),
        P(None, "ctx"),
    )
    out_specs = (P(("dp", "ctx"), None), P(None, ("dp", "ctx")))
    return jax.shard_map(
        on_device, mesh=mesh, in_specs=in_specs, out_specs=out_specs, check_vma=False
    )
```

```python
import math

import jax
import jax.numpy as jnp
from jax import lax
from jax.experimental import pallas as pl
from jax.experimental.pallas import tpu as pltpu
from jax.sharding import PartitionSpec as P

MESH = pl.DeviceIdType.MESH
HEADS = 2
HEAD_DIM = 128
NX, NC, NZ, NY = 4, 2, 8, 4
ROWS = 256
HALF = 128
FEATURES = HEADS * HEAD_DIM
MODEL = 4096
PARTS = NX * NC
PIECE = FEATURES // PARTS
REACH = 4
MASKED = -1e30
SCALE = 1.0 / math.sqrt(HEAD_DIM)
SCALE2 = SCALE * math.log2(math.e)
AROUND = [(0, 0), (0, 1), (1, 0)]
JUMP = 2


def attend_kernel(
    q_in, k_in, v_in, doc_in, w_in,
    att, w_all, lse_ref,
    q_all, k_all, vt_all, v_own, doc_q, doc_k, key_doc,
    acc, stat, o_send, o_recv, relay_k, relay_v, kept, kept_fade,
    loc_sem, kv_ss, kv_rs, a_ss, a_rs, one_ss, one_rs, o_ss, o_rs,
):
    dp = lax.axis_index("dp")
    ctx = lax.axis_index("ctx")
    x, core = dp // NC, lax.rem(dp, NC)
    z, y = ctx // NY, lax.rem(ctx, NY)

    def at(dx=0, flip=False, dz=0, dy=0):
        x_to = lax.rem(x + dx + NX, NX)
        core_to = 1 - core if flip else core
        z_to = lax.rem(z + dz + NZ, NZ)
        y_to = lax.rem(y + dy + NY, NY)
        return (x_to * NC + core_to, z_to * NY + y_to)

    def remote(src, dst, ss, rs, to):
        return pltpu.make_async_remote_copy(
            src_ref=src, dst_ref=dst, send_sem=ss, recv_sem=rs, device_id=to, device_id_type=MESH
        )

    barrier = pltpu.get_barrier_semaphore()
    partners = [at(dz=d) for d in range(1, NZ)]
    partners += [at(dy=d) for d in range(1, NY)]
    partners += [at(dx=d) for d in range(1, NX)]
    partners += [at(flip=True)]
    for to in partners:
        pl.semaphore_signal(barrier, inc=1, device_id=to, device_id_type=MESH)

    piece = pl.ds(pl.multiple_of(dp * PIECE, PIECE), PIECE)
    z_cols = pl.ds(pl.multiple_of(z * 128, 128), 128)
    locals_ = [
        pltpu.make_async_copy(k_in.at[:, 0:128], k_all.at[0, 0], loc_sem.at[0]),
        pltpu.make_async_copy(k_in.at[:, 128:256], k_all.at[0, 1], loc_sem.at[1]),
        pltpu.make_async_copy(doc_in, doc_q.at[0], loc_sem.at[2]),
        pltpu.make_async_copy(w_in.at[piece], w_all.at[0, piece, z_cols], loc_sem.at[3]),
        pltpu.make_async_copy(v_in, v_own, loc_sem.at[4]),
        pltpu.make_async_copy(q_in, q_all.at[0], loc_sem.at[5]),
    ]
    for copy in locals_:
        copy.start()

    def wait_bytes(like, sem):
        pltpu.make_async_copy(like, like, sem).wait()

    def kv_copy(h, k, part):
        ref = (k_all, vt_all)[part]
        return remote(
            ref.at[k, h], ref.at[k + 1, h],
            kv_ss.at[k], kv_rs.at[h, k, part], at(dz=1),
        )

    def advance(h, k, part):
        @pl.when(z >= k)
        def _():
            kv_copy(h, k - 1, part).wait_recv()

        if k > (REACH - 2 if (h, part) in AROUND else REACH - 1):
            return

        @pl.when((z >= k) & (z < NZ - 1))
        def _():
            kv_copy(h, k, part).start()

    def around_out(h, part):
        return remote(
            (k_all, vt_all)[part].at[0, h], (relay_k, relay_v)[part].at[h],
            a_ss.at[0], a_rs.at[AROUND.index((h, part))], at(dz=-JUMP),
        )

    def around_in(h, part):
        return remote(
            (relay_k, relay_v)[part].at[h], (k_all, vt_all)[part].at[REACH, h],
            a_ss.at[1], kv_rs.at[h, REACH - 1, part], at(dz=-JUMP),
        )

    sends_around = z < NZ - REACH

    def send_around(index):
        @pl.when(sends_around)
        def _():
            around_out(*AROUND[index]).start()

    def relay_around(index, here):
        @pl.when(here)
        def _():
            around_out(*AROUND[index]).wait_recv()
            around_in(*AROUND[index]).start()

    relays_low = (z < NZ - REACH - JUMP) | (z == NZ - 1)
    relays_high = (z >= NZ - JUMP) & (z < NZ - 1)

    def group(index, pairs):
        return [remote(src, dst, one_ss.at[index], one_rs.at[index], to) for src, dst, to in pairs]

    q_copies = group(1 + 1, [(q_in, q_all.at[d], at(dy=d)) for d in range(1, NY)])
    dy_copies = group(3, [(doc_in, doc_q.at[d], at(dy=d)) for d in range(1, NY)])
    dz_copies = group(4, [(doc_in, doc_k.at[k - 1], at(dz=k)) for k in range(1, REACH + 1)])
    own_piece = w_all.at[0, piece, z_cols]
    w1_copies = group(5, [(own_piece, own_piece, at(dz=d)) for d in range(1, NZ)])
    own_column = w_all.at[0, piece]
    w2_copies = group(6, [(own_column, w_all.at[d, piece], at(dy=d)) for d in range(1, NY)])
    w3_first = group(7, [(own_column, own_column, at(dx=d)) for d in range(1, NX)])
    others = w_all.at[1:NY, piece]
    w3_rest = group(8, [(others, others, at(dx=d)) for d in (1, NX - 1)])
    far_part = lax.rem(x + NX // 2, NX) * NC + core
    far_rows = pl.ds(pl.multiple_of(far_part * PIECE, PIECE), PIECE)
    w2_far = group(0, [(w_all.at[0, far_rows], w_all.at[d, far_rows], at(dy=d)) for d in range(1, NY)])

    def part_rows(dx):
        part = lax.rem(x - dx + NX, NX) * NC + core
        return w_all.at[:, pl.ds(pl.multiple_of(part * PIECE, PIECE), PIECE)]

    w4_copies = group(9, [(part_rows(d), part_rows(d), at(flip=True)) for d in range(NX)])

    def weight_over_y():
        wait_bytes(w_all.at[0, 0 : (NZ - 1) * PIECE, 0:128], one_rs.at[5])
        for copy in w2_copies + w3_first:
            copy.start()

    def weight_over_x():
        wait_bytes(w_all.at[1:NY, piece], one_rs.at[6])
        for copy in w3_rest:
            copy.start()
        wait_bytes(w_all.at[1:NY, piece], one_rs.at[7])
        for copy in w2_far:
            copy.start()
        w4_copies[0].start()

    def weight_over_core():
        wait_bytes(w_all.at[1:NY, 0 : 2 * PIECE], one_rs.at[8])
        for d in (1, NX - 1):
            w4_copies[d].start()
        wait_bytes(w_all.at[1:NY, piece], one_rs.at[0])
        w4_copies[NX // 2].start()

    o_copies = [
        [
            remote(o_send.at[h, d - 1], o_recv.at[h, d - 1], o_ss.at[h], o_rs.at[h], at(dy=-d))
            for d in range(1, NY)
        ]
        for h in range(HEADS)
    ]

    def turned_docs(row):
        return jnp.broadcast_to(row, (128, ROWS)).T

    def half_weights(h, k, d, cols, causal):
        head = pl.ds(h * HEAD_DIM if isinstance(h, int) else pl.multiple_of(h * HEAD_DIM, HEAD_DIM), HEAD_DIM)
        scores = lax.dot_general(
            k_all[k, h], q_all[d, cols, head],
            (((1,), (1,)), ((), ())), preferred_element_type=jnp.float32,
        )
        visible = key_doc[k] == doc_q[d, :, cols]
        if causal:
            key_row = lax.broadcasted_iota(jnp.int32, (ROWS, HALF), 0)
            query_row = lax.broadcasted_iota(jnp.int32, (ROWS, HALF), 1) + cols.start
            visible = visible & (key_row <= query_row)
        scores = jnp.where(visible, scores, MASKED)
        old = stat[d, h, 0:1, cols]
        top = jnp.maximum(jnp.max(scores, axis=0, keepdims=True), old)
        weights = jnp.exp2((scores - top) * SCALE2)
        fade = jnp.exp2((old - top) * SCALE2)
        total = stat[d, h, 1:2, cols] * fade + jnp.sum(weights, axis=0, keepdims=True)
        stat[d, h, 1:2, cols] = total
        stat[d, h, 0:1, cols] = top
        return weights.astype(jnp.bfloat16), fade

    def half_sum(h, k, d, cols, weights, fade):
        product = jnp.dot(vt_all[k, h], weights, preferred_element_type=jnp.float32)
        acc[d, h, :, cols] = acc[d, h, :, cols] * fade + product

    halves = [slice(start, start + HALF) for start in range(0, ROWS, HALF)]

    def tile(h, k, d, causal=False):
        for cols in halves:
            half_sum(h, k, d, cols, *half_weights(h, k, d, cols, causal))

    def tile_weights(h, k, d):
        for cols in halves:
            kept[d, :, cols], kept_fade[d, 0:1, cols] = half_weights(h, k, d, cols, False)

    def tile_sum(h, k, d):
        for cols in halves:
            half_sum(h, k, d, cols, kept[d, :, cols], kept_fade[d, 0:1, cols])

    def thirds(row):
        high = row.astype(jnp.bfloat16).astype(jnp.float32)
        rest = row - high
        middle = rest.astype(jnp.bfloat16).astype(jnp.float32)
        return [high, middle, rest - middle]

    def give_back(h, d):
        rows = thirds(stat[d, h, 0:1]) + thirds(stat[d, h, 1:2])
        rows += [jnp.zeros((16 - len(rows), ROWS), jnp.float32)]
        o_send[h, d - 1, 0:HEAD_DIM] = acc[d, h].astype(jnp.bfloat16)
        o_send[h, d - 1, HEAD_DIM : HEAD_DIM + 16] = jnp.concatenate(rows, axis=0).astype(jnp.bfloat16)
        o_copies[h][d - 1].start()

    locals_[0].wait()
    locals_[1].wait()
    pl.semaphore_wait(barrier, len(partners))

    def send_own(h, part):
        @pl.when(z < NZ - 1)
        def _():
            kv_copy(h, 0, part).start()

    send_own(0, 0)
    send_around(0)
    for copy in dz_copies + dy_copies:
        copy.start()
    locals_[3].wait()
    locals_[4].wait()
    v_turned = v_own[...].T
    for h in range(HEADS):
        vt_all[0, h] = v_turned[h * HEAD_DIM : (h + 1) * HEAD_DIM]
    send_own(0, 1)
    for d in (2, 1, 3):
        q_copies[d - 1].start()
    send_own(1, 1)
    for copy in w1_copies:
        copy.start()
    send_around(1)

    locals_[2].wait()
    locals_[5].wait()
    acc[...] = jnp.zeros_like(acc)
    stat[:, :, 0:1] = jnp.full((NY, HEADS, 1, ROWS), MASKED, jnp.float32)
    stat[:, :, 1:2] = jnp.zeros((NY, HEADS, 1, ROWS), jnp.float32)
    key_doc[0] = turned_docs(doc_q[0])
    for h in range(HEADS):
        tile(h, 0, 0, causal=True)

    advance(0, 1, 0)
    advance(0, 1, 1)
    send_own(1, 0)
    send_around(2)
    wait_bytes(doc_k, one_rs.at[4])
    for k in range(1, REACH + 1):
        @pl.when(z >= k)
        def _(k=k):
            key_doc[k] = turned_docs(doc_k[k - 1])
    relay_around(0, relays_low)
    advance(0, 2, 0)
    advance(1, 1, 1)
    weight_over_y()
    relay_around(1, relays_low)
    wait_bytes(q_all.at[1:NY], one_rs.at[2])
    wait_bytes(doc_q.at[1:NY], one_rs.at[3])

    for low in range(NY - 1):
        @pl.when(y == low)
        def _(low=low):
            for d in range(low + 1, NY):
                for h in range(HEADS):
                    tile(h, 0, d)

    def give_back_early(h):
        for d in range(NY - 1, 0, -1):
            @pl.when(y < d)
            def _(d=d):
                give_back(h, d)

    def far(h, step):
        for high in range(1, NY):
            @pl.when((z >= REACH) & (y == high))
            def _(high=high):
                for d in range(1, high + 1):
                    step(h, REACH, d)

    def give_back_late(h):
        for d in range(NY - 1, 0, -1):
            @pl.when(y >= d)
            def _(d=d):
                give_back(h, d)

    def far_own(h):
        @pl.when(z >= REACH)
        def _():
            tile(h, REACH, 0)

    arrivals = [
        [(0, 2, 1), (1, 1, 0)],
        [],
        [(1, 2, 1)],
        [(0, 3, 0), (0, 3, 1)],
        [(1, 2, 0)],
    ]

    def unit(u, carry):
        for index, chunks in enumerate(arrivals):
            @pl.when(u == index)
            def _(index=index, chunks=chunks):
                if index == 2:
                    weight_over_x()
                    for chunk in range(len(AROUND)):
                        relay_around(chunk, relays_high)
                for chunk in chunks:
                    advance(*chunk)
                if index == 0:
                    relay_around(2, relays_low)
                if index == 4:
                    give_back_early(0)

        past = [0, (u + 4) // 5, (u + 3) // 5, u // 3, u // 4, u // 5]
        h = past[2] - past[3] + past[4]
        k = 1 + past[1] - past[2] + 2 * past[3] - past[4] + past[5]

        @pl.when(z >= k)
        def _():
            for d in range(NY):
                tile(h, k, d)

        return carry

    lax.fori_loop(0, len(arrivals), unit, 0)
    advance(1, 3, 1)
    advance(0, REACH, 0)
    advance(0, REACH, 1)
    far(0, tile)
    give_back_late(0)
    advance(1, 3, 0)

    def near_last(first):
        for high in range(NY):
            @pl.when((z >= REACH - 1) & (y == high))
            def _(high=high):
                for d in range(1, high + 1) if first else [0, *range(high + 1, NY)]:
                    tile(1, REACH - 1, d)

    near_last(True)

    advance(1, REACH, 0)
    far(1, tile_weights)
    advance(1, REACH, 1)
    for d in range(NY - 1, 0, -1):
        @pl.when((z >= REACH) & (y >= d))
        def _(d=d):
            tile_sum(1, REACH, d)

        @pl.when(y >= d)
        def _(d=d):
            give_back(1, d)
    near_last(False)
    give_back_early(1)
    far_own(0)
    far_own(1)
    weight_over_core()

    for h in range(HEADS):
        wait_bytes(o_recv.at[h], o_rs.at[h])
        tops, sums = [stat[0, h, 0:1]], [stat[0, h, 1:2]]
        for d in range(NY - 1):
            rows = o_recv[h, d, HEAD_DIM : HEAD_DIM + 16].astype(jnp.float32)
            tops.append(rows[0:1] + rows[1:2] + rows[2:3])
            sums.append(rows[3:4] + rows[4:5] + rows[5:6])
        top = tops[0]
        for other in tops[1:]:
            top = jnp.maximum(top, other)
        shares = [jnp.exp2((one - top) * SCALE2) for one in tops]
        total = sums[0] * shares[0]
        for d in range(1, NY):
            total = total + sums[d] * shares[d]
        lse_ref[h : h + 1] = top * SCALE + jnp.log(total)
        value = acc[0, h] * (shares[0] / total)
        for d in range(1, NY):
            value = value + o_recv[h, d - 1, 0:HEAD_DIM].astype(jnp.float32) * (shares[d] / total)
        att[:, h * HEAD_DIM : (h + 1) * HEAD_DIM] = value.astype(jnp.bfloat16).T

    wait_bytes(w_all.at[:, 0 : NX * PIECE], one_rs.at[9])

    for k in range(REACH):
        @pl.when((z >= k) & (z < NZ - 1))
        def _(k=k):
            wait_bytes(k_all.at[0:2] if k < REACH - 1 else k_all.at[0, 0], kv_ss.at[k])

    @pl.when(sends_around)
    def _():
        wait_bytes(k_all.at[0:3, 0], a_ss.at[0])

    @pl.when(relays_low | relays_high)
    def _():
        wait_bytes(k_all.at[0:3, 0], a_ss.at[1])

    wait_bytes(q_all.at[1:NY], one_ss.at[2])
    wait_bytes(doc_q.at[1:NY], one_ss.at[3])
    wait_bytes(doc_k, one_ss.at[4])
    wait_bytes(w_all.at[0, 0 : (NZ - 1) * PIECE, 0:128], one_ss.at[5])
    wait_bytes(w_all.at[1:NY, piece], one_ss.at[6])
    wait_bytes(w_all.at[1:NY, piece], one_ss.at[7])
    wait_bytes(w_all.at[1:NY, 0 : 2 * PIECE], one_ss.at[8])
    wait_bytes(w_all.at[1:NY, piece], one_ss.at[0])
    wait_bytes(w_all.at[:, 0 : NX * PIECE], one_ss.at[9])
    for h in range(HEADS):
        wait_bytes(o_send.at[h], o_ss.at[h])


def project_kernel(att, w_all, lse_in, out_ref, lse_ref, stage, sems):
    lse_copy = pltpu.make_async_copy(lse_in, lse_ref, sems.at[NZ])
    lse_copy.start()
    attended = att[...]
    y = lax.rem(lax.axis_index("ctx"), NY)
    writes = []
    width = NY * 128
    for block in range(NZ):
        weight = jnp.concatenate(
            [w_all[lax.rem(y - c + NY, NY), :, block * 128 : (block + 1) * 128] for c in range(NY)], axis=1
        )
        cols = slice(block * width, (block + 1) * width)
        stage[:, cols] = jnp.dot(
            attended, weight, preferred_element_type=jnp.float32
        ).astype(jnp.bfloat16)
        write = pltpu.make_async_copy(stage.at[:, cols], out_ref.at[:, cols], sems.at[block])
        write.start()
        writes.append(write)
    for write in writes + [lse_copy]:
        write.wait()


def on_device(queries, keys, values, document_ids, output_weight):
    bf16, f32, i32 = jnp.bfloat16, jnp.float32, jnp.int32
    dma = pltpu.SemaphoreType.DMA
    anywhere = pl.BlockSpec(memory_space=pl.ANY)
    local = pl.BlockSpec(memory_space=pltpu.VMEM)
    attended, weight, lse = pl.pallas_call(
        attend_kernel,
        out_shape=(
            jax.ShapeDtypeStruct((ROWS, FEATURES), bf16),
            jax.ShapeDtypeStruct((NY, FEATURES, NZ * 128), bf16),
            jax.ShapeDtypeStruct((HEADS, ROWS), f32),
        ),
        in_specs=[pl.BlockSpec(memory_space=pltpu.HBM)] * 5,
        out_specs=(local, anywhere, local),
        scratch_shapes=[
            pltpu.VMEM((NY, ROWS, FEATURES), bf16),
            pltpu.VMEM((REACH + 1, HEADS, ROWS, HEAD_DIM), bf16),
            pltpu.VMEM((REACH + 1, HEADS, HEAD_DIM, ROWS), bf16),
            pltpu.VMEM((ROWS, FEATURES), bf16),
            pltpu.VMEM((NY, 1, ROWS), i32),
            pltpu.VMEM((REACH, 1, ROWS), i32),
            pltpu.VMEM((REACH + 1, ROWS, 128), i32),
            pltpu.VMEM((NY, HEADS, HEAD_DIM, ROWS), f32),
            pltpu.VMEM((NY, HEADS, 2, ROWS), f32),
            pltpu.VMEM((HEADS, NY - 1, HEAD_DIM + 16, ROWS), bf16),
            pltpu.VMEM((HEADS, NY - 1, HEAD_DIM + 16, ROWS), bf16),
            pltpu.VMEM((HEADS, ROWS, HEAD_DIM), bf16),
            pltpu.VMEM((HEADS, HEAD_DIM, ROWS), bf16),
            pltpu.VMEM((NY, ROWS, ROWS), bf16),
            pltpu.VMEM((NY, 1, ROWS), f32),
            dma((6,)), dma((REACH,)), dma((HEADS, REACH, 2)), dma((2,)), dma((3,)),
            dma((10,)), dma((10,)), dma((HEADS,)), dma((HEADS,)),
        ],
        compiler_params=pltpu.CompilerParams(
            collective_id=0, has_side_effects=True, vmem_limit_bytes=32 << 20
        ),
    )(*[
        pltpu.with_memory_space_constraint(one, pltpu.HBM)
        for one in (queries, keys, values, document_ids.reshape(1, ROWS), output_weight)
    ])
    return pl.pallas_call(
        project_kernel,
        out_shape=(
            jax.ShapeDtypeStruct((ROWS, MODEL), bf16),
            jax.ShapeDtypeStruct((HEADS, ROWS), f32),
        ),
        in_specs=[local, local, anywhere],
        out_specs=(anywhere, anywhere),
        scratch_shapes=[pltpu.VMEM((ROWS, MODEL), bf16), dma((NZ + 1,))],
        compiler_params=pltpu.CompilerParams(vmem_limit_bytes=32 << 20),
    )(attended, weight, lse)


def solution(mesh):
    in_specs = (
        P(("dp", "ctx"), None),
        P(("dp", "ctx"), None),
        P(("dp", "ctx"), None),
        P(("dp", "ctx")),
        P(None, "ctx"),
    )
    out_specs = (P(("dp", "ctx"), None), P(None, ("dp", "ctx")))
    return jax.shard_map(
        on_device, mesh=mesh, in_specs=in_specs, out_specs=out_specs, check_vma=False
    )
```
